512 devices in a mesh: outer: 64 (over y_hi, x, z), inner: 8 (over y_lo, core).
Axes of the slice: x: 4, y: 8 (y_hi: 2, y_lo: 4; y = y_hi * 4 + y_lo), z: 8, core: 2. Of those that a mesh axis runs over, the one named last changes fastest.
Arguments:
- queries: bfloat16 [262144, 768], P(('outer', 'inner')), may hold values from -6 to 6
- keys: bfloat16 [262144, 768], P(('outer', 'inner')), may hold values from -6 to 6
- values: bfloat16 [262144, 768], P(('outer', 'inner')), may hold values from -6 to 6
- offsets: int32 [12], replicated, may hold values from 0 to 7
- w_out: bfloat16 [768, 768], replicated, may hold values from -0.21875 to 0.21875
Outputs:
- mixed: bfloat16 [262144, 768], P(('outer', 'inner'))
The draws below stay inside these ranges and needn't reach their ends.
All inputs are finite; a program needn't handle non-finite values.
Results may differ from the reference program's by a relative error of at most 0.0056.
Values may be sent and summed in bfloat16 or wider, within the bound.
A program may use at most 64 MiB of HBM per device.

```python
import math
import jax
import jax.numpy as jnp
from jax import lax

D = 768
HEAD_COUNT = 12
DH = 64
TOK_DEV = 512
LOCAL_SPAN = 256
PICKED_TOKENS = 512
TOKENS = 262144
LEVEL_ONE_DILATE = 8
LEVEL_TWO_DILATE = 64
LEVEL_THREE_GAP = 512


def draw_queries(key, part):
    key = jax.random.fold_in(key, 11)
    field = 1.5 * jax.random.normal(key, (TOKENS, HEAD_COUNT * DH), jnp.float32)
    return jnp.clip(field, -6.0, 6.0).astype(jnp.bfloat16)


def draw_keys(key, part):
    key = jax.random.fold_in(key, 23)
    noise = jax.random.normal(key, (TOKENS, HEAD_COUNT * DH), jnp.float32)
    field = 1.5 * noise
    return jnp.clip(field, -6.0, 6.0).astype(jnp.bfloat16)


def draw_offsets(key, part):
    key = jax.random.fold_in(key, 37)
    first_key, second_key = jax.random.split(key)
    base = jax.random.randint(first_key, (HEAD_COUNT,), 0, LEVEL_ONE_DILATE, dtype=jnp.int32)
    order = jax.random.permutation(second_key, HEAD_COUNT).astype(jnp.int32)
    heads_iota = jnp.arange(HEAD_COUNT, dtype=jnp.int32)
    base = jnp.where(heads_iota == order[0], jnp.zeros((), jnp.int32), base)
    base = jnp.where(heads_iota == order[1], jnp.full((), LEVEL_ONE_DILATE - 1, jnp.int32), base)
    return base.astype(jnp.int32)


def level_of(own_key, dims, cuts, least, top_value):
    def one(position, shards_of):
        heights = jax.random.uniform(jax.random.fold_in(jax.random.fold_in(own_key, 6), position), (shards_of,), jnp.float32, least / len(cuts), top_value / len(cuts))
        return jnp.repeat(jnp.exp(heights), dims[position] // shards_of).reshape((-1,) + (1,) * (len(dims) - position - 1))

    gain = one(*cuts[0])
    for cut in cuts[1:]:
        gain = gain * one(*cut)
    return gain


def normal_values(rng, dims, width, reach, cuts=(), kind=jnp.bfloat16):
    drawn = width * jax.random.normal(rng, dims, jnp.float32)
    if cuts:
        drawn = drawn * level_of(rng, dims, cuts, -0.22, 0.18)
    return jnp.clip(drawn, -reach, reach).astype(kind)


def setup_inputs(seed: int = 0) -> dict:
    splits = jax.random.split(jax.random.key(seed), 6)
    queries = draw_queries(jax.random.fold_in(splits[5], 71), 0)
    keys = draw_keys(jax.random.fold_in(splits[5], 71), 0)
    values = normal_values(splits[2], (TOKENS, D), 1.0, 6.0, ((0, 512),))
    offsets = draw_offsets(jax.random.fold_in(splits[5], 71), 0)
    w_out = normal_values(splits[4], (D, D), D ** -0.5, 0.21875)
    return dict(queries=queries, keys=keys, values=values, offsets=offsets, w_out=w_out)


NEG = -1e+30

def pick(field, dilation_step, offsets):
    count, heads, depth = field.shape
    grid = field.reshape(count // dilation_step, dilation_step, heads, depth)
    chosen = jnp.arange(dilation_step, dtype=jnp.int32)[:, None] == offsets[None, :]
    return lax.optimization_barrier(jnp.sum(jnp.where(chosen[None, :, :, None], grid, jnp.zeros((), field.dtype)), axis=1))

def spread(vals, dilation_step, offsets, fill):
    chosen = jnp.arange(dilation_step, dtype=jnp.int32)[:, None] == offsets[None, :]
    shape = (1, dilation_step, offsets.shape[0]) + (1,) * (vals.ndim - 2)
    wide = jnp.where(chosen.reshape(shape), vals[:, None], jnp.asarray(fill, jnp.float32))
    return wide.reshape((vals.shape[0] * dilation_step,) + vals.shape[1:])

def attend(queries, keys, values):
    scale = 1.0 / math.sqrt(DH)
    scores = jnp.einsum('phd,shd->hps', queries.astype(jnp.float32), keys.astype(jnp.float32)) * scale
    top = lax.optimization_barrier(jnp.max(scores, axis=2))
    expo = jnp.exp(scores - top[:, :, None])
    total = lax.optimization_barrier(jnp.sum(expo, axis=2))
    weights = expo.astype(jnp.bfloat16)
    numer = jnp.einsum('hps,shd->phd', weights.astype(jnp.float32), values.astype(jnp.float32))
    return (top.T, total.T, numer)

def combine(parts):
    peak = parts[0][0]
    for part in parts[1:]:
        peak = jnp.maximum(peak, part[0])
    denom = jnp.zeros(peak.shape, jnp.float32)
    summed = jnp.zeros(parts[0][2].shape, jnp.float32)
    for top, total, numer in parts:
        factor = jnp.exp(top - peak)
        denom = denom + factor * total
        summed = summed + factor[:, :, None] * numer
    return summed / denom[:, :, None]

def level_results(q_all, k_all, v_all, offsets, dilation_step):
    q_sel = pick(q_all, dilation_step, offsets)
    k_sel = pick(k_all, dilation_step, offsets)
    v_sel = pick(v_all, dilation_step, offsets)
    count = q_sel.shape[0]

    def one_segment(index):
        start = (index * PICKED_TOKENS).astype(jnp.int32)
        return attend(lax.dynamic_slice_in_dim(q_sel, start, PICKED_TOKENS, 0), lax.dynamic_slice_in_dim(k_sel, start, PICKED_TOKENS, 0), lax.dynamic_slice_in_dim(v_sel, start, PICKED_TOKENS, 0))
    top, total, numer = lax.map(one_segment, jnp.arange(count // PICKED_TOKENS, dtype=jnp.int32))
    return (top.reshape(count, HEAD_COUNT), total.reshape(count, HEAD_COUNT), numer.reshape(count, HEAD_COUNT, DH))

def local_part(q_blk, k_blk, v_blk):
    segments = TOK_DEV // LOCAL_SPAN
    shape = (segments, LOCAL_SPAN, HEAD_COUNT, DH)
    top, total, numer = lax.map(lambda trio: attend(trio[0], trio[1], trio[2]), (q_blk.reshape(shape), k_blk.reshape(shape), v_blk.reshape(shape)))
    return (top.reshape(TOK_DEV, HEAD_COUNT), total.reshape(TOK_DEV, HEAD_COUNT), numer.reshape(TOK_DEV, HEAD_COUNT, DH))

def reference(queries, keys, values, offsets, w_out):
    q_all = queries.reshape(TOKENS, HEAD_COUNT, DH)
    k_all = keys.reshape(TOKENS, HEAD_COUNT, DH)
    v_all = values.reshape(TOKENS, HEAD_COUNT, DH)
    dilation_steps = (LEVEL_ONE_DILATE, LEVEL_TWO_DILATE, LEVEL_THREE_GAP)
    results = [level_results(q_all, k_all, v_all, offsets, dilation_step) for dilation_step in dilation_steps]

    def one_block(index):
        start = (index * TOK_DEV).astype(jnp.int32)
        q_blk = lax.dynamic_slice_in_dim(q_all, start, TOK_DEV, 0)
        k_blk = lax.dynamic_slice_in_dim(k_all, start, TOK_DEV, 0)
        v_blk = lax.dynamic_slice_in_dim(v_all, start, TOK_DEV, 0)
        parts = [local_part(q_blk, k_blk, v_blk)]
        for dilation_step, (top, total, numer) in zip(dilation_steps, results):
            count = TOK_DEV // dilation_step
            begin = (index * count).astype(jnp.int32)
            parts.append((spread(lax.dynamic_slice_in_dim(top, begin, count, 0), dilation_step, offsets, NEG), spread(lax.dynamic_slice_in_dim(total, begin, count, 0), dilation_step, offsets, 0.0), spread(lax.dynamic_slice_in_dim(numer, begin, count, 0), dilation_step, offsets, 0.0)))
        attended = combine(parts).astype(jnp.bfloat16).reshape(TOK_DEV, HEAD_COUNT * DH)
        return jnp.dot(attended, w_out, preferred_element_type=jnp.float32).astype(jnp.bfloat16)
    blocks = lax.map(one_block, jnp.arange(TOKENS // TOK_DEV, dtype=jnp.int32))
    return blocks.reshape(TOKENS, D)
```

```python
import math

import jax
import jax.numpy as jnp
from jax import lax
from jax.experimental import pallas as pl
from jax.experimental.pallas import tpu as pltpu
from jax.sharding import PartitionSpec as P

MESH = pl.DeviceIdType.MESH
F32, BF16 = jnp.float32, jnp.bfloat16
LANES = 128
HALF = 64
SPAN = 256
TOK = 512
PICK = 64
PAIRS = 6
COEF = 0.125 * math.log2(math.e)


def iota(shape, dim):
    return lax.broadcasted_iota(jnp.int32, shape, dim)


def nn(a, b):
    return lax.dot_general(a, b, (((1,), (0,)), ((), ())), preferred_element_type=F32)


def nt(a, b):
    return lax.dot_general(a, b, (((1,), (1,)), ((), ())), preferred_element_type=F32)


def tn(a, b):
    return lax.dot_general(a, b, (((0,), (0,)), ((), ())), preferred_element_type=F32)


def onehot(cond):
    return jnp.where(cond, jnp.float32(1), jnp.float32(0)).astype(BF16)


def eye(n):
    return onehot(iota((n, n), 0) == iota((n, n), 1))


def stacked(q):
    low = iota(q.shape, 1) < HALF
    wide = q.astype(F32)
    return jnp.concatenate([jnp.where(low, wide, 0.0), jnp.where(low, 0.0, wide)], axis=0).astype(BF16)


def split3(x):
    hi = x.astype(BF16).astype(F32)
    rest = x - hi
    mid = rest.astype(BF16).astype(F32)
    return hi, mid, rest - mid


def flipped(v):
    up = nt(eye(LANES), v)
    return jnp.concatenate([up, jnp.ones((16, v.shape[0]), F32)], axis=0).astype(BF16)


def attend_t(keys, queries, v_up):
    s = nt(keys, queries)
    top = jnp.max(s, axis=0, keepdims=True)
    w = jnp.exp2((s - top) * COEF).astype(BF16)
    return top, nn(v_up, w)


def kernel(off_ref, q_ref, k_ref, v_ref, out_ref, pick2, pick1, buf1, buf2, buf3, three, ret1, got1, ret2, got2,
           spread, v_up, sel_loc, s_a1, r_a1, s_a2, r_a2, s_b, r_b, s_c, r_c, s_d, r_d, s_e, r_e, s_f, r_f):
    outer = lax.axis_index("outer")
    i = lax.axis_index("inner")
    z = lax.rem(outer, 8)
    xy = outer // 8
    pair = i - 1
    owner = jnp.logical_and(i >= 1, i <= PAIRS)

    def of_inner(k):
        return (outer, lax.rem(i + k, 8))

    def of_z(k):
        return (xy * 8 + lax.rem(z + k, 8), i)

    def of_xy(k):
        return (lax.rem(xy + k, 8) * 8 + z, i)

    barrier = pltpu.get_barrier_semaphore()
    for k in range(1, 8):
        for at in (of_inner, of_z, of_xy):
            pl.semaphore_signal(barrier, inc=1, device_id=at(k), device_id_type=MESH)

    def cols(p):
        return slice(p * LANES, (p + 1) * LANES)

    def copy(src, dst, s, r, to):
        return pltpu.make_async_remote_copy(src_ref=src, dst_ref=dst, send_sem=s, recv_sem=r, device_id=to,
                                            device_id_type=MESH)

    low8 = iota((8, LANES), 1) < HALF
    for p in range(PAIRS):
        row = iota((16, TOK), 0)
        offs = jnp.where(row < 8, off_ref[2 * p], off_ref[2 * p + 1])
        hot = onehot(iota((16, TOK), 1) == PICK * lax.rem(row, 8) + offs)
        rows = []
        for ref in (k_ref, v_ref):
            got = nn(hot, ref[:, cols(p)])
            rows.append(jnp.where(low8, got[0:8], got[8:16]))
        pick2[p] = jnp.concatenate(rows, axis=0).astype(BF16)

    low64 = iota((PICK, LANES), 1) < HALF
    for p in range(PAIRS):
        row = iota((LANES, TOK), 0)
        offs = jnp.where(row < HALF, off_ref[2 * p], off_ref[2 * p + 1])
        hot = onehot(iota((LANES, TOK), 1) == 8 * lax.rem(row, HALF) + offs)
        for n, ref in enumerate((k_ref, v_ref, q_ref)):
            got = nn(hot, ref[:, cols(p)])
            pick1[p, n * PICK : (n + 1) * PICK] = jnp.where(low64, got[0:64], got[64:128]).astype(BF16)

    pl.semaphore_wait(barrier, 21)

    def send_a1(p):
        return copy(pick2.at[p], buf2.at[z, i], s_a1.at[p], r_a1.at[i], (outer, p + 1))

    def send_a2(p):
        return copy(pick1.at[p], buf1.at[i], s_a2.at[p], r_a2.at[i], (outer, p + 1))

    for p in range(PAIRS):
        @pl.when(i != p + 1)
        def _(p=p):
            send_a1(p).start()

        @pl.when(i == p + 1)
        def _(p=p):
            buf2[z, i] = pick2[p]

    for p in range(PAIRS):
        @pl.when(i != p + 1)
        def _(p=p):
            send_a2(p).start()

        @pl.when(i == p + 1)
        def _(p=p):
            buf1[i] = pick1[p]

    def local(p):
        v_up[p] = flipped(v_ref[:, cols(p)])
        for g in range(TOK // SPAN):
            rows = slice(g * SPAN, (g + 1) * SPAN)
            _, o = attend_t(k_ref[rows, cols(p)], stacked(q_ref[rows, cols(p)]), v_up[p, :, rows])
            a = o[0:64, 0:SPAN] / o[128:129, 0:SPAN]
            b = o[64:128, 0 + SPAN : 2 * SPAN] / o[128:129, SPAN : 2 * SPAN]
            up = jnp.concatenate([a, b], axis=0).astype(BF16)
            flat = nt(eye(SPAN), up)
            offs = jnp.where(iota((SPAN, LANES), 1) < HALF, off_ref[2 * p], off_ref[2 * p + 1])
            on = lax.rem(iota((SPAN, LANES), 0), 8) == offs
            out_ref[rows, cols(p)] = jnp.where(on, 0.0, flat).astype(BF16)

    lane = iota((1, LANES), 1)

    def local_selected(p):
        qs = stacked(pick1[p, 2 * PICK : 3 * PICK])
        parts = []
        for g in range(TOK // SPAN):
            rows = slice(g * SPAN, (g + 1) * SPAN)
            parts.append(attend_t(k_ref[rows, cols(p)], qs, v_up[p, :, rows]))
        first = lax.rem(lane, HALF) < PICK // 2
        top = jnp.where(first, parts[0][0], parts[1][0])
        o = jnp.where(first, parts[0][1], parts[1][1])
        sel_loc[p, 0:64] = jnp.where(lane < HALF, o[0:64], o[64:128])
        sel_loc[p, 64:72] = jnp.broadcast_to(top, (8, LANES))
        sel_loc[p, 72:80] = jnp.broadcast_to(o[128:129], (8, LANES))
        col = iota((TOK, LANES), 1)
        offs = jnp.where(col < HALF, off_ref[2 * p], off_ref[2 * p + 1])
        spread[p] = onehot(iota((TOK, LANES), 0) == 8 * lax.rem(col, HALF) + offs)

    def z_send(buf, s, r, k):
        return copy(buf.at[z], buf.at[z], s.at[k], r.at[z], of_z(k))

    def z_recv(buf, s, r, k):
        other = lax.rem(z + k, 8)
        return copy(buf.at[other], buf.at[other], s.at[k], r.at[other], of_z(k))

    local(0)
    local(1)

    @pl.when(owner)
    def _():
        for k in range(1, 8):
            src = lax.rem(i + k, 8)
            copy(pick2.at[0], buf2.at[z, src], s_a1.at[0], r_a1.at[src], of_inner(k)).wait_recv()
        rows = buf2[z].reshape(LANES, LANES)
        r, c = iota((16, LANES), 0), iota((16, LANES), 1)
        hot = onehot(c == 16 * lax.rem(r, 8) + 8 * (r // 8))
        buf3[xy, z] = nn(hot, rows).astype(BF16)
        for k in (4, 3, 5, 2, 6, 1, 7):
            copy(buf3.at[xy, z], buf3.at[xy, z], s_c.at[k], r_c.at[z], of_z(k)).start()
        for k in (4, 3, 5, 2, 6, 1, 7):
            z_send(buf2, s_b, r_b, k).start()

    local(2)
    local(3)

    @pl.when(owner)
    def _():
        for k in range(1, 8):
            other = lax.rem(z + k, 8)
            copy(buf3.at[xy, z], buf3.at[xy, other], s_c.at[k], r_c.at[other], of_z(k)).wait_recv()
        for k in range(1, 8):
            copy(buf3.at[xy], buf3.at[xy], s_d.at[k], r_d.at[xy], of_xy(k)).start()

    local(4)
    local(5)

    def level_one():
        keys = buf1[:, 0:PICK].reshape(8 * PICK, LANES)
        values = flipped(buf1[:, PICK : 2 * PICK].reshape(8 * PICK, LANES))
        for n in range(4):
            qs = jnp.concatenate([stacked(buf1[2 * n, 2 * PICK :]), stacked(buf1[2 * n + 1, 2 * PICK :])], axis=0)
            top, o = attend_t(keys, qs, values)
            total = o[128:129]
            parts = list(split3(top)) + list(split3(total)) + [jnp.zeros((10, 2 * LANES), F32)]
            both = lax.rem(iota((1, 2 * LANES), 1), LANES) < HALF
            whole = jnp.concatenate([jnp.where(both, o[0:64], o[64:128])] + parts, axis=0).astype(BF16)
            ret1[2 * n] = whole[:, 0:LANES]
            ret1[2 * n + 1] = whole[:, LANES:]

    def ret_send(ret, got, s, r, k):
        dst = lax.rem(i + k, 8)
        return copy(ret.at[dst], got.at[pair], s.at[k], r.at[pair], of_inner(k))

    @pl.when(owner)
    def _():
        for k in range(1, 8):
            src = lax.rem(i + k, 8)
            copy(pick1.at[0], buf1.at[src], s_a2.at[0], r_a2.at[src], of_inner(k)).wait_recv()
        level_one()
        for k in range(1, 8):
            ret_send(ret1, got1, s_e, r_e, k).start()
        got1[pair] = ret1[i]

    for p in range(PAIRS):
        local_selected(p)

    def keys_values(buf):
        wide = buf[...].reshape(64, 16, LANES).astype(F32)
        return (wide[:, 0:8].reshape(512, LANES).astype(BF16), wide[:, 8:16].reshape(512, LANES).astype(BF16))

    def attend_rows(queries, buf):
        keys, values = keys_values(buf)
        s = nt(queries, keys)
        top = jnp.max(s, axis=1, keepdims=True)
        e = jnp.exp2((s - top) * COEF)
        return top, jnp.sum(e, axis=1, keepdims=True), nn(e.astype(BF16), values)

    @pl.when(owner)
    def _():
        r, c = iota((LANES, TOK), 0), iota((LANES, TOK), 1)
        hot = onehot(c == PICK * (r // 16) + 8 * lax.rem(r, 8))
        q2 = nn(hot, buf1[:, 2 * PICK :].reshape(TOK, LANES))
        r, c = iota((LANES, LANES), 0), iota((LANES, LANES), 1)
        mine = (lax.rem(r, 16) < 8) == (c < HALF)
        q2 = jnp.where(mine, q2, 0.0).astype(BF16)
        for k in range(1, 8):
            z_recv(buf2, s_b, r_b, k).wait_recv()
        top2, total2, numer2 = attend_rows(q2, buf2)
        for k in range(1, 8):
            other = lax.rem(xy + k, 8)
            copy(buf3.at[xy], buf3.at[other], s_d.at[k], r_d.at[other], of_xy(k)).wait_recv()
        top3, total3, numer3 = attend_rows(q2, buf3)
        on = lax.rem(iota((LANES, 1), 0), 8) == 0
        peak = jnp.maximum(top2, jnp.where(on, top3, top2))
        f2 = jnp.exp2((top2 - peak) * COEF)
        f3 = jnp.where(on, jnp.exp2((jnp.where(on, top3, peak) - peak) * COEF), 0.0)
        total = f2 * total2 + f3 * total3
        whole = f2 * numer2 + f3 * numer3
        at = lax.rem(c, HALF)
        for n, x in enumerate(split3(peak) + split3(total)):
            whole = jnp.where(jnp.logical_and(jnp.logical_not(mine), at == n), x, whole)
        whole = jnp.where(jnp.logical_or(mine, at < 6), whole, 0.0)
        ret2[...] = whole.astype(BF16).reshape(8, 16, LANES)
        for k in range(1, 8):
            ret_send(ret2, got2, s_f, r_f, k).start()
        got2[pair] = ret2[i]

    for p in range(PAIRS):
        @pl.when(i != p + 1)
        def _(p=p):
            copy(ret1.at[0], got1.at[p], s_e.at[1], r_e.at[p], (outer, p + 1)).wait_recv()

    for p in range(PAIRS):
        @pl.when(i != p + 1)
        def _(p=p):
            copy(ret2.at[0], got2.at[p], s_f.at[1], r_f.at[p], (outer, p + 1)).wait_recv()

    r, c = iota((16, LANES), 0), iota((16, LANES), 1)
    hot = onehot(jnp.logical_and(r // 8 == c // HALF, lax.rem(c, HALF) == 8 * lax.rem(r, 8)))
    first = lane < HALF
    on = lax.rem(lane, 8) == 0
    for p in range(PAIRS):
        x = tn(got2[p], hot)
        numer2 = jnp.where(first, x[0:64], x[64:128])
        st = jnp.where(first, x[64:72], x[0:8])
        top2 = (st[0:1] + st[1:2]) + st[2:3]
        total2 = (st[3:4] + st[4:5]) + st[5:6]
        y = got1[p].astype(F32)
        numer1 = y[0:64]
        top1 = (y[64:65] + y[65:66]) + y[66:67]
        total1 = (y[67:68] + y[68:69]) + y[69:70]
        top0 = sel_loc[p, 64:65]
        total0 = sel_loc[p, 72:73]
        top2 = jnp.where(on, top2, top0)
        peak = jnp.maximum(jnp.maximum(top0, top1), top2)
        f0 = jnp.exp2((top0 - peak) * COEF)
        f1 = jnp.exp2((top1 - peak) * COEF)
        f2 = jnp.where(on, jnp.exp2((top2 - peak) * COEF), 0.0)
        total = f0 * total0 + f1 * total1 + f2 * total2
        done = (f0 * sel_loc[p, 0:64] + f1 * numer1 + f2 * numer2) / total
        both = jnp.concatenate([jnp.where(first, done, 0.0), jnp.where(first, 0.0, done)], axis=0).astype(BF16)
        back = nt(spread[p], both)
        out_ref[:, cols(p)] = (out_ref[:, cols(p)].astype(F32) + back).astype(BF16)

    for p in range(PAIRS):
        @pl.when(i != p + 1)
        def _(p=p):
            send_a1(p).wait_send()
            send_a2(p).wait_send()

    @pl.when(owner)
    def _():
        for k in range(1, 8):
            copy(buf3.at[xy, z], buf3.at[xy, z], s_c.at[k], r_c.at[z], of_z(k)).wait_send()
            z_send(buf2, s_b, r_b, k).wait_send()
            copy(buf3.at[xy], buf3.at[xy], s_d.at[k], r_d.at[xy], of_xy(k)).wait_send()
            ret_send(ret1, got1, s_e, r_e, k).wait_send()
            ret_send(ret2, got2, s_f, r_f, k).wait_send()


def shards(queries, keys, values, offsets, w_out):
    vmem = pl.BlockSpec(memory_space=pltpu.VMEM)
    dma = pltpu.SemaphoreType.DMA
    attended = pl.pallas_call(
        kernel,
        out_shape=jax.ShapeDtypeStruct(queries.shape, BF16),
        in_specs=[pl.BlockSpec(memory_space=pltpu.SMEM), vmem, vmem, vmem],
        out_specs=vmem,
        scratch_shapes=[
            pltpu.VMEM((PAIRS, 16, LANES), BF16),
            pltpu.VMEM((PAIRS, 3 * PICK, LANES), BF16),
            pltpu.VMEM((8, 3 * PICK, LANES), BF16),
            pltpu.VMEM((8, 8, 16, LANES), BF16),
            pltpu.VMEM((8, 8, 16, LANES), BF16),
            pltpu.VMEM((16, LANES), BF16),
            pltpu.VMEM((8, 80, LANES), BF16),
            pltpu.VMEM((PAIRS, 80, LANES), BF16),
            pltpu.VMEM((8, 16, LANES), BF16),
            pltpu.VMEM((PAIRS, 16, LANES), BF16),
            pltpu.VMEM((PAIRS, TOK, LANES), BF16),
            pltpu.VMEM((PAIRS, 144, TOK), BF16),
            pltpu.VMEM((PAIRS, 80, LANES), F32),
        ] + [dma((8,))] * 14,
        compiler_params=pltpu.CompilerParams(
            collective_id=0, has_side_effects=True, vmem_limit_bytes=48 * 1024 * 1024
        ),
    )(offsets, queries, keys, values)
    return jnp.dot(attended, w_out, preferred_element_type=F32).astype(BF16)


def solution(mesh):
    rows = P(("outer", "inner"), None)
    return jax.shard_map(
        shards, mesh=mesh, in_specs=(rows, rows, rows, P(), P()), out_specs=rows, check_vma=False
    )
```

```python
import math

import jax
import jax.numpy as jnp
from jax import lax
from jax.experimental import pallas as pl
from jax.experimental.pallas import tpu as pltpu
from jax.sharding import PartitionSpec as P

MESH = pl.DeviceIdType.MESH
F32, BF16 = jnp.float32, jnp.bfloat16
LANES = 128
HALF = 64
SPAN = 256
TOK = 512
PICK = 64
PAIRS = 6
NEG = -1e30
COEF = 0.125 * math.log2(math.e)


def mod(x, n):
    return x & (n - 1)


def div(x, n):
    return x >> (n.bit_length() - 1)


def iota(shape, dim):
    return lax.broadcasted_iota(jnp.int32, shape, dim)


def nn(a, b):
    return lax.dot_general(a, b, (((1,), (0,)), ((), ())), preferred_element_type=F32)


def nt(a, b):
    return lax.dot_general(a, b, (((1,), (1,)), ((), ())), preferred_element_type=F32)


def tn(a, b):
    return lax.dot_general(a, b, (((0,), (0,)), ((), ())), preferred_element_type=F32)


def onehot(cond):
    return jnp.where(cond, jnp.float32(1), jnp.float32(0)).astype(BF16)


def eye(n):
    return onehot(iota((n, n), 0) == iota((n, n), 1))


def stacked(q):
    low = iota(q.shape, 1) < HALF
    wide = q.astype(F32)
    return jnp.concatenate([jnp.where(low, wide, 0.0), jnp.where(low, 0.0, wide)], axis=0).astype(BF16)


def split3(x):
    hi = x.astype(BF16).astype(F32)
    rest = x - hi
    mid = rest.astype(BF16).astype(F32)
    return hi, mid, rest - mid


def flipped(v):
    up = nt(eye(LANES), v)
    return jnp.concatenate([up, jnp.ones((16, v.shape[0]), F32)], axis=0).astype(BF16)


def attend_t(keys, queries, v_up):
    s = nt(keys, queries)
    top = jnp.max(s, axis=0, keepdims=True)
    w = jnp.exp2((s - top) * COEF).astype(BF16)
    return top, nn(v_up, w)


def kernel(off_ref, q_hbm, k_hbm, v_hbm, out_ref, q_ref, k_ref, v_ref, k_few, v_few, q_few, pick2, pick1, buf1, buf2,
           ret1, got1, ret2, got2, kv3, q3, part3, got3, spread, v_up, sel_loc, s_in, s_a1, r_a1, s_a2, r_a2, s_b, r_b,
           s_e, r_e, s_f, r_f, s_g, r_g, s_q, r_q, s_p, r_p):
    outer = lax.axis_index("outer")
    i = lax.axis_index("inner")
    z = mod(outer, 8)
    xy = div(outer, 8)
    far = div(outer, 32)
    cell = z * 4 + mod(xy, 4)
    ring = far * 8 + i
    pair = i - 1
    owner = jnp.logical_and(i >= 1, i <= PAIRS)
    early = z < 4
    first_pairs = jnp.maximum(PAIRS - div(3 * z + 1, 2), 0)
    second_pairs = jnp.maximum(first_pairs, 1)
    third_pairs = jnp.maximum(first_pairs, 3)

    loads = [pltpu.make_async_copy(hbm.at[:, pl.ds(0, 16)], few, s_in.at[n])
             for n, (hbm, few) in enumerate(((k_hbm, k_few), (v_hbm, v_few)))]
    loads += [pltpu.make_async_copy(q_hbm.at[0, pl.ds(0, 16)], q_few, s_in.at[2])]
    loads += [pltpu.make_async_copy(hbm, ref, s_in.at[3 + n])
              for n, (hbm, ref) in enumerate(((k_hbm, k_ref), (v_hbm, v_ref), (q_hbm, q_ref)))]
    for load in loads:
        load.start()

    def of_inner(k):
        return (outer, mod(i + k, 8))

    def of_z(k):
        return (xy * 8 + mod(z + k, 8), i)

    def at_cell(c):
        return (far * 32 + mod(c, 4) * 8 + div(c, 4), i)

    def of_cell(k):
        return at_cell(mod(cell + k, 32))

    def of_ring(k):
        at = mod(ring + k, 16)
        return (div(at, 8) * 32 + mod(outer, 32), mod(at, 8))

    barrier = pltpu.get_barrier_semaphore()
    for k in range(1, 16):
        pl.semaphore_signal(barrier, inc=1, device_id=of_ring(k), device_id_type=MESH)
    for k in range(1, 32):
        pl.semaphore_signal(barrier, inc=1, device_id=of_cell(k), device_id_type=MESH)

    def cols(p):
        if isinstance(p, int):
            return slice(p * LANES, (p + 1) * LANES)
        return pl.ds(pl.multiple_of(p * LANES, LANES), LANES)

    def rows_of(ref, g, p):
        return ref[g * 4 : (g + 1) * 4, :, cols(p)].reshape(SPAN, LANES)

    def all_of(ref, p):
        return ref[:, :, cols(p)].reshape(TOK, LANES)

    def copy(src, dst, s, r, to):
        return pltpu.make_async_remote_copy(src_ref=src, dst_ref=dst, send_sem=s, recv_sem=r, device_id=to,
                                            device_id_type=MESH)

    for load in loads[:3]:
        load.wait()

    def one_row(block):
        x = block.astype(F32)[0:8]
        at = iota((8, LANES), 0)
        rows = jnp.zeros((8, LANES), F32)
        for p in range(PAIRS):
            offs = jnp.where(iota((8, LANES), 1) < HALF, off_ref[2 * p], off_ref[2 * p + 1])
            row = jnp.sum(jnp.where(at == offs, x[:, cols(p)], 0.0), axis=0, keepdims=True)
            rows = jnp.where(at == p, row, rows)
        return rows

    kv3[ring] = jnp.concatenate([one_row(k_few[0]), one_row(v_few[0])], axis=0).astype(BF16)
    q3[cell] = one_row(q_few[...])

    low8 = iota((8, LANES), 1) < HALF
    for p in range(PAIRS):
        row = iota((16, LANES), 0)
        offs = jnp.where(row < 8, off_ref[2 * p], off_ref[2 * p + 1])
        hot = onehot(iota((16, LANES), 1) == 16 * mod(row, 8) + offs)
        rows = []
        for ref in (k_few, v_few):
            got = nn(hot, ref[:, :, cols(p)].reshape(LANES, LANES))
            rows.append(jnp.where(low8, got[0:8], got[8:16]))
        pick2[p] = jnp.concatenate(rows, axis=0).astype(BF16)

    def select(p):
        row = iota((LANES, TOK), 0)
        low = iota((PICK, LANES), 1) < HALF
        offs = jnp.where(row < HALF, off_ref[2 * p], off_ref[2 * p + 1])
        hot = onehot(iota((LANES, TOK), 1) == 8 * mod(row, HALF) + offs)
        for n, ref in enumerate((k_ref, v_ref, q_ref)):
            got = nn(hot, all_of(ref, p))
            pick1[p, n * PICK : (n + 1) * PICK] = jnp.where(low, got[0:64], got[64:128]).astype(BF16)

    def own(p):
        v_up[p] = flipped(all_of(v_ref, p))
        for g in range(TOK // SPAN):
            rows = slice(g * SPAN, (g + 1) * SPAN)
            _, o = attend_t(rows_of(k_ref, g, p), stacked(rows_of(q_ref, g, p)), v_up[p, :, rows])
            a = o[0:64, 0:SPAN] / o[128:129, 0:SPAN]
            b = o[64:128, 0 + SPAN : 2 * SPAN] / o[128:129, SPAN : 2 * SPAN]
            up = jnp.concatenate([a, b], axis=0).astype(BF16)
            flat = nt(eye(SPAN), up)
            offs = jnp.where(iota((SPAN, LANES), 1) < HALF, off_ref[2 * p], off_ref[2 * p + 1])
            on = mod(iota((SPAN, LANES), 0), 8) == offs
            out_ref[rows, cols(p)] = jnp.where(on, 0.0, flat).astype(BF16)

    lane = iota((1, LANES), 1)

    def local_selected(p):
        qs = stacked(pick1[p, 2 * PICK : 3 * PICK])
        parts = []
        for g in range(TOK // SPAN):
            rows = slice(g * SPAN, (g + 1) * SPAN)
            parts.append(attend_t(rows_of(k_ref, g, p), qs, v_up[p, :, rows]))
        first = mod(lane, HALF) < PICK // 2
        top = jnp.where(first, parts[0][0], parts[1][0])
        o = jnp.where(first, parts[0][1], parts[1][1])
        sel_loc[p, 0:64] = jnp.where(lane < HALF, o[0:64], o[64:128])
        sel_loc[p, 64:72] = jnp.broadcast_to(top, (8, LANES))
        sel_loc[p, 72:80] = jnp.broadcast_to(o[128:129], (8, LANES))
        col = iota((TOK, LANES), 1)
        offs = jnp.where(col < HALF, off_ref[2 * p], off_ref[2 * p + 1])
        spread[p] = onehot(iota((TOK, LANES), 0) == 8 * mod(col, HALF) + offs)

    def local(p):
        own(p)
        local_selected(p)

    def loop(begin, end, body):
        lax.fori_loop(begin, end, lambda p, _: (body(p), 0)[1], 0)

    @pl.when(early)
    def _():
        for load in loads[3:]:
            load.wait()
        for p in range(PAIRS):
            select(p)
        loop(0, first_pairs, local)

    pl.semaphore_wait(barrier, 46)

    def ring_copy(k):
        return copy(kv3.at[ring], kv3.at[ring], s_g.at[k], r_g.at[ring], of_ring(k))

    def query_copy(k):
        return copy(q3.at[cell], q3.at[cell], s_q.at[k], r_q.at[cell], of_cell(k))

    def part_copy(to):
        return copy(part3.at[to], got3.at[cell], s_p.at[to], r_p.at[cell], at_cell(to))

    def others(half, body):
        for k in range(16):
            at = 16 * half + mod(cell + k, 16)
            if k:
                body(at)
            else:
                pl.when(div(cell, 16) != half)(lambda: body(at))

    for k in range(1, 16):
        ring_copy(k).start()

    def send_a1(p):
        return copy(pick2.at[p], buf2.at[z, i], s_a1.at[p], r_a1.at[i], (outer, p + 1))

    def send_a2(p):
        return copy(pick1.at[p], buf1.at[i], s_a2.at[p], r_a2.at[i], (outer, p + 1))

    for p in range(PAIRS):
        @pl.when(i != p + 1)
        def _(p=p):
            send_a1(p).start()

        @pl.when(i == p + 1)
        def _(p=p):
            buf2[z, i] = pick2[p]

    for k in range(1, 32):
        query_copy(k).start()

    @pl.when(jnp.logical_not(early))
    def _():
        for load in loads[3:]:
            load.wait()
        for p in range(PAIRS):
            select(p)

    for p in range(PAIRS):
        @pl.when(i != p + 1)
        def _(p=p):
            send_a2(p).start()

        @pl.when(i == p + 1)
        def _(p=p):
            buf1[i] = pick1[p]

    def z_send(buf, s, r, k):
        return copy(buf.at[z], buf.at[z], s.at[k], r.at[z], of_z(k))

    def z_recv(buf, s, r, k):
        other = mod(z + k, 8)
        return copy(buf.at[other], buf.at[other], s.at[k], r.at[other], of_z(k))

    loop(first_pairs, second_pairs, local)

    @pl.when(owner)
    def _():
        for k in range(1, 8):
            src = mod(i + k, 8)
            copy(pick2.at[0], buf2.at[z, src], s_a1.at[0], r_a1.at[src], of_inner(k)).wait_recv()
        for k in (4, 3, 5, 2, 6, 1, 7):
            z_send(buf2, s_b, r_b, k).start()

    r, c = iota((2 * LANES, LANES), 0), iota((2 * LANES, LANES), 1)
    hot_q = onehot(jnp.logical_and(div(r, 16) == div(c, 8), div(mod(r, 16), 2) == mod(c, 8)))
    head4 = mod(r, 16)
    mine4 = mod(head4, 2) == div(c, HALF)
    key4 = div(c, 16) == div(head4, 2)
    spot4 = mod(c, HALF)

    def fourth(half, rows4):
        def arrived(at):
            copy(q3.at[at], q3.at[at], s_q.at[0], r_q.at[at], at_cell(at)).wait_recv()

        others(half, arrived)
        mine = slice(16 * half, 16 * half + 16)
        queries4 = nn(hot_q, q3[mine].reshape(LANES, LANES).astype(BF16))
        queries4 = jnp.where(mine4, queries4, 0.0).astype(BF16)
        s = jnp.where(key4, nt(queries4, rows4[0:LANES]), NEG)
        top = jnp.max(s, axis=1, keepdims=True)
        e = jnp.exp2((s - top) * COEF)
        total = jnp.sum(e, axis=1, keepdims=True)
        stats = jnp.where(spot4 == 0, top, jnp.where(spot4 == 1, total, 0.0))
        part3[mine] = jnp.where(mine4, nn(e.astype(BF16), rows4[LANES:]), stats).reshape(16, 16, LANES)
        others(half, lambda at: part_copy(at).start())

    for k in range(1, 16):
        at = mod(ring + k, 16)
        copy(kv3.at[at], kv3.at[at], s_g.at[k], r_g.at[at], of_ring(k)).wait_recv()
    r, c = iota((2 * LANES, 2 * LANES), 0), iota((2 * LANES, 2 * LANES), 1)
    hot = onehot(c == 16 * mod(r, 16) + 8 * div(r, LANES) + div(mod(r, LANES), 16))
    rows4 = nn(hot, kv3[...].reshape(2 * LANES, LANES)).astype(BF16)
    fourth(0, rows4)
    loop(second_pairs, third_pairs, local)
    fourth(1, rows4)
    got3[cell] = part3[cell]

    def level_one():
        keys = buf1[:, 0:PICK].reshape(8 * PICK, LANES)
        values = flipped(buf1[:, PICK : 2 * PICK].reshape(8 * PICK, LANES))
        for n in range(4):
            qs = jnp.concatenate([stacked(buf1[2 * n, 2 * PICK :]), stacked(buf1[2 * n + 1, 2 * PICK :])], axis=0)
            top, o = attend_t(keys, qs, values)
            total = o[128:129]
            parts = list(split3(top)) + list(split3(total)) + [jnp.zeros((10, 2 * LANES), F32)]
            both = mod(iota((1, 2 * LANES), 1), LANES) < HALF
            whole = jnp.concatenate([jnp.where(both, o[0:64], o[64:128])] + parts, axis=0).astype(BF16)
            ret1[2 * n] = whole[:, 0:LANES]
            ret1[2 * n + 1] = whole[:, LANES:]

    def ret_send(ret, got, s, r, k):
        dst = mod(i + k, 8)
        return copy(ret.at[dst], got.at[pair], s.at[k], r.at[pair], of_inner(k))

    @pl.when(owner)
    def _():
        for k in range(1, 8):
            src = mod(i + k, 8)
            copy(pick1.at[0], buf1.at[src], s_a2.at[0], r_a2.at[src], of_inner(k)).wait_recv()
        level_one()
        for k in range(1, 8):
            ret_send(ret1, got1, s_e, r_e, k).start()
        got1[pair] = ret1[i]

    def keys_values(buf):
        wide = buf[...].reshape(64, 16, LANES).astype(F32)
        return (wide[:, 0:8].reshape(512, LANES).astype(BF16), wide[:, 8:16].reshape(512, LANES).astype(BF16))

    def attend_rows(queries, buf):
        keys, values = keys_values(buf)
        s = nt(queries, keys)
        top = jnp.max(s, axis=1, keepdims=True)
        e = jnp.exp2((s - top) * COEF)
        return top, jnp.sum(e, axis=1, keepdims=True), nn(e.astype(BF16), values)

    @pl.when(owner)
    def _():
        r, c = iota((LANES, TOK), 0), iota((LANES, TOK), 1)
        hot = onehot(c == PICK * div(r, 16) + 8 * mod(r, 8))
        q2 = nn(hot, buf1[:, 2 * PICK :].reshape(TOK, LANES))
        r, c = iota((LANES, LANES), 0), iota((LANES, LANES), 1)
        mine = (mod(r, 16) < 8) == (c < HALF)
        q2 = jnp.where(mine, q2, 0.0).astype(BF16)
        for k in range(1, 8):
            z_recv(buf2, s_b, r_b, k).wait_recv()
        top2, total2, numer2 = attend_rows(q2, buf2)
        at = mod(c, HALF)
        whole = numer2
        for n, x in enumerate(split3(top2) + split3(total2)):
            whole = jnp.where(jnp.logical_and(jnp.logical_not(mine), at == n), x, whole)
        whole = jnp.where(jnp.logical_or(mine, at < 6), whole, 0.0)
        ret2[...] = whole.astype(BF16).reshape(8, 16, LANES)
        for k in range(1, 8):
            ret_send(ret2, got2, s_f, r_f, k).start()
        got2[pair] = ret2[i]

    loop(third_pairs, PAIRS, local)

    for p in range(PAIRS):
        @pl.when(i != p + 1)
        def _(p=p):
            copy(ret1.at[0], got1.at[p], s_e.at[1], r_e.at[p], (outer, p + 1)).wait_recv()

    for p in range(PAIRS):
        @pl.when(i != p + 1)
        def _(p=p):
            copy(ret2.at[0], got2.at[p], s_f.at[1], r_f.at[p], (outer, p + 1)).wait_recv()

    for k in range(1, 32):
        at = mod(cell + k, 32)
        copy(part3.at[at], got3.at[at], s_p.at[k], r_p.at[at], of_cell(k)).wait_recv()
    x = got3[...]
    lane3 = iota((32, 16, LANES), 2)
    other = mod(iota((32, 16, LANES), 1), 2) != div(lane3, HALF)
    spot = mod(lane3, HALF)
    top = jnp.max(jnp.where(jnp.logical_and(other, spot == 0), x, NEG), axis=2, keepdims=True)
    total = jnp.sum(jnp.where(jnp.logical_and(other, spot == 1), x, 0.0), axis=2, keepdims=True)
    peak = jnp.max(top, axis=0, keepdims=True)
    f = jnp.exp2((top - peak) * COEF)
    numer = jnp.sum(f * x, axis=0)
    total = jnp.sum(f * total, axis=0)
    r, c = iota((16, LANES), 0), iota((16, LANES), 1)
    mine = mod(r, 2) == div(c, HALF)
    spot = mod(c, HALF)
    for n, v in enumerate(split3(peak.reshape(16, 1)) + split3(total)):
        numer = jnp.where(jnp.logical_and(jnp.logical_not(mine), spot == n), v, numer)
    rows4 = jnp.where(jnp.logical_or(mine, spot < 6), numer, 0.0).astype(BF16)
    r, c = iota((16, PAIRS * LANES), 0), iota((16, PAIRS * LANES), 1)
    all4 = tn(rows4, onehot(jnp.logical_and(r == div(c, HALF), mod(c, HALF) == 0)))

    r, c = iota((16, LANES), 0), iota((16, LANES), 1)
    hot = onehot(jnp.logical_and(div(r, 8) == div(c, HALF), mod(c, HALF) == 8 * mod(r, 8)))
    first = lane < HALF
    on = mod(lane, 8) == 0
    on4 = mod(lane, HALF) == 0

    def unpacked(x):
        st = jnp.where(first, x[64:72], x[0:8])
        return (st[0:1] + st[1:2]) + st[2:3], (st[3:4] + st[4:5]) + st[5:6], jnp.where(first, x[0:64], x[64:128])

    for p in range(PAIRS):
        top2, total2, numer2 = unpacked(tn(got2[p], hot))
        top3, total3, numer3 = unpacked(all4[:, cols(p)])
        y = got1[p].astype(F32)
        numer1 = y[0:64]
        top1 = (y[64:65] + y[65:66]) + y[66:67]
        total1 = (y[67:68] + y[68:69]) + y[69:70]
        top0 = sel_loc[p, 64:65]
        total0 = sel_loc[p, 72:73]
        top2 = jnp.where(on, top2, top0)
        top3 = jnp.where(on4, top3, top0)
        peak = jnp.maximum(jnp.maximum(top0, top1), jnp.maximum(top2, top3))
        f0 = jnp.exp2((top0 - peak) * COEF)
        f1 = jnp.exp2((top1 - peak) * COEF)
        f2 = jnp.where(on, jnp.exp2((top2 - peak) * COEF), 0.0)
        f3 = jnp.where(on4, jnp.exp2((top3 - peak) * COEF), 0.0)
        total = f0 * total0 + f1 * total1 + f2 * total2 + f3 * total3
        done = (f0 * sel_loc[p, 0:64] + f1 * numer1 + f2 * numer2 + f3 * numer3) / total
        both = jnp.concatenate([jnp.where(first, done, 0.0), jnp.where(first, 0.0, done)], axis=0).astype(BF16)
        back = nt(spread[p], both)
        out_ref[:, cols(p)] = (out_ref[:, cols(p)].astype(F32) + back).astype(BF16)

    for k in range(1, 16):
        ring_copy(k).wait_send()
    for k in range(1, 32):
        query_copy(k).wait_send()
    for half in range(2):
        others(half, lambda at: part_copy(at).wait_send())
    for p in range(PAIRS):
        @pl.when(i != p + 1)
        def _(p=p):
            send_a1(p).wait_send()
            send_a2(p).wait_send()

    @pl.when(owner)
    def _():
        for k in range(1, 8):
            z_send(buf2, s_b, r_b, k).wait_send()
            ret_send(ret1, got1, s_e, r_e, k).wait_send()
            ret_send(ret2, got2, s_f, r_f, k).wait_send()


def shards(queries, keys, values, offsets, w_out):
    hbm = pl.BlockSpec(memory_space=pltpu.HBM)
    shape = (8, 64, queries.shape[1])
    dma = pltpu.SemaphoreType.DMA
    attended = pl.pallas_call(
        kernel,
        out_shape=jax.ShapeDtypeStruct(queries.shape, BF16),
        in_specs=[pl.BlockSpec(memory_space=pltpu.SMEM), hbm, hbm, hbm],
        out_specs=pl.BlockSpec(memory_space=pltpu.VMEM),
        scratch_shapes=[pltpu.VMEM(shape, BF16)] * 3 + [pltpu.VMEM((8, 16, shape[2]), BF16)] * 2 + [
            pltpu.VMEM((16, shape[2]), BF16),
            pltpu.VMEM((PAIRS, 16, LANES), BF16),
            pltpu.VMEM((PAIRS, 3 * PICK, LANES), BF16),
            pltpu.VMEM((8, 3 * PICK, LANES), BF16),
            pltpu.VMEM((8, 8, 16, LANES), BF16),
            pltpu.VMEM((8, 80, LANES), BF16),
            pltpu.VMEM((PAIRS, 80, LANES), BF16),
            pltpu.VMEM((8, 16, LANES), BF16),
            pltpu.VMEM((PAIRS, 16, LANES), BF16),
            pltpu.VMEM((16, 16, LANES), BF16),
            pltpu.VMEM((32, 8, LANES), F32),
            pltpu.VMEM((32, 16, LANES), F32),
            pltpu.VMEM((32, 16, LANES), F32),
            pltpu.VMEM((PAIRS, TOK, LANES), BF16),
            pltpu.VMEM((PAIRS, 144, TOK), BF16),
            pltpu.VMEM((PAIRS, 80, LANES), F32),
        ] + [dma((6,))] + [dma((8,))] * 10 + [dma((16,))] * 2 + [dma((32,))] * 4,
        compiler_params=pltpu.CompilerParams(
            collective_id=0, has_side_effects=True, vmem_limit_bytes=53 * 1024 * 1024
        ),
    )(offsets, queries.reshape(shape), keys.reshape(shape), values.reshape(shape))
    return jnp.dot(attended, w_out, preferred_element_type=F32).astype(BF16)


def solution(mesh):
    rows = P(("outer", "inner"), None)
    return jax.shard_map(
        shards, mesh=mesh, in_specs=(rows, rows, rows, P(), P()), out_specs=rows, check_vma=False
    )
```

```python
import math

import jax
import jax.numpy as jnp
from jax import lax
from jax.experimental import pallas as pl
from jax.experimental.pallas import tpu as pltpu
from jax.sharding import PartitionSpec as P

MESH = pl.DeviceIdType.MESH
F32, BF16 = jnp.float32, jnp.bfloat16
LANES = 128
HALF = 64
SPAN = 256
TOK = 512
PICK = 64
PAIRS = 6
NEG = -1e30
COEF = 0.125 * math.log2(math.e)


def mod(x, n):
    return x & (n - 1)


def div(x, n):
    return x >> (n.bit_length() - 1)


def iota(shape, dim):
    return lax.broadcasted_iota(jnp.int32, shape, dim)


def nn(a, b):
    return lax.dot_general(a, b, (((1,), (0,)), ((), ())), preferred_element_type=F32)


def nt(a, b):
    return lax.dot_general(a, b, (((1,), (1,)), ((), ())), preferred_element_type=F32)


def tn(a, b):
    return lax.dot_general(a, b, (((0,), (0,)), ((), ())), preferred_element_type=F32)


def onehot(cond):
    return jnp.where(cond, jnp.float32(1), jnp.float32(0)).astype(BF16)


def eye(n):
    return onehot(iota((n, n), 0) == iota((n, n), 1))


def stacked(q):
    low = iota(q.shape, 1) < HALF
    wide = q.astype(F32)
    return jnp.concatenate([jnp.where(low, wide, 0.0), jnp.where(low, 0.0, wide)], axis=0).astype(BF16)


def split3(x):
    hi = x.astype(BF16).astype(F32)
    rest = x - hi
    mid = rest.astype(BF16).astype(F32)
    return hi, mid, rest - mid


def flipped(v):
    up = nt(eye(LANES), v)
    return jnp.concatenate([up, jnp.ones((16, v.shape[0]), F32)], axis=0).astype(BF16)


def attend_t(keys, queries, v_up):
    s = nt(keys, queries)
    top = jnp.max(s, axis=0, keepdims=True)
    w = jnp.exp2((s - top) * COEF).astype(BF16)
    return top, nn(v_up, w)


def kernel(off_ref, q_hbm, k_hbm, v_hbm, out_ref, q_ref, k_ref, v_ref, k_few, v_few, q_few, pick2, pick1, buf1, buf2,
           ret1, got1, ret2, got2, rows3, ring3, all3, ret3, got3, spread, v_up, sel_loc, s_in, s_a1, r_a1, s_a2, r_a2, s_b, r_b,
           s_e, r_e, s_f, r_f, s_g, r_g, s_q, r_q, s_p, r_p, later):
    outer = lax.axis_index("outer")
    i = lax.axis_index("inner")
    z = mod(outer, 8)
    xy = div(outer, 8)
    far = div(outer, 32)
    cell = z * 4 + mod(xy, 4)
    ring = far * 8 + i
    head = far * PAIRS + i - 1
    odd = mod(head, 2) == 1
    pair = i - 1
    owner = jnp.logical_and(i >= 1, i <= PAIRS)
    first_pairs = jnp.clip(7 - z, 1, PAIRS)
    second_pairs = jnp.maximum(first_pairs, 4)

    loads = [pltpu.make_async_copy(hbm.at[:, pl.ds(0, 16)], few, s_in.at[n])
             for n, (hbm, few) in enumerate(((k_hbm, k_few), (v_hbm, v_few)))]
    loads += [pltpu.make_async_copy(q_hbm.at[0, pl.ds(0, 16)], q_few, s_in.at[2])]
    loads += [pltpu.make_async_copy(hbm, ref, s_in.at[3 + n])
              for n, (hbm, ref) in enumerate(((k_hbm, k_ref), (v_hbm, v_ref), (q_hbm, q_ref)))]
    for load in loads:
        load.start()

    def of_inner(k):
        return (outer, mod(i + k, 8))

    def of_z(k):
        return (xy * 8 + mod(z + k, 8), i)

    def at_cell(c):
        return (far * 32 + mod(c, 4) * 8 + div(c, 4), i)

    def of_cell(k):
        return at_cell(mod(cell + k, 32))

    def of_ring(k):
        at = mod(ring + k, 16)
        return (div(at, 8) * 32 + mod(outer, 32), mod(at, 8))

    barrier = pltpu.get_barrier_semaphore()
    for k in range(1, 16):
        pl.semaphore_signal(barrier, inc=1, device_id=of_ring(k), device_id_type=MESH)

    def cells(body, chosen):
        for k in range(1, 32):
            at = mod(cell + k, 32)
            pl.when(chosen(div(at, 4)))(lambda: body(at))

    cells(lambda at: pl.semaphore_signal(barrier, inc=1, device_id=at_cell(at), device_id_type=MESH), lambda w: w >= z)

    def cols(p):
        if isinstance(p, int):
            return slice(p * LANES, (p + 1) * LANES)
        return pl.ds(pl.multiple_of(p * LANES, LANES), LANES)

    def rows_of(ref, g, p):
        return ref[g * 4 : (g + 1) * 4, :, cols(p)].reshape(SPAN, LANES)

    def all_of(ref, p):
        return ref[:, :, cols(p)].reshape(TOK, LANES)

    def copy(src, dst, s, r, to):
        return pltpu.make_async_remote_copy(src_ref=src, dst_ref=dst, send_sem=s, recv_sem=r, device_id=to,
                                            device_id_type=MESH)

    for load in loads[:3]:
        load.wait()

    def one_row(block):
        x = block.astype(F32)[0:8]
        at = iota((8, LANES), 0)
        rows = jnp.zeros((8, LANES), F32)
        for p in range(PAIRS):
            offs = jnp.where(iota((8, LANES), 1) < HALF, off_ref[2 * p], off_ref[2 * p + 1])
            row = jnp.sum(jnp.where(at == offs, x[:, cols(p)], 0.0), axis=0, keepdims=True)
            rows = jnp.where(at == p, row, rows)
        return rows

    key_row, value_row, query_row = one_row(k_few[0]), pltpu.roll(one_row(v_few[0]), HALF, 1), one_row(q_few[...])
    at, low = iota((8, LANES), 0), iota((8, LANES), 1) < HALF
    for h in range(2 * PAIRS):
        p = div(h, 2)
        own_half = low if h % 2 == 0 else jnp.logical_not(low)
        both = jnp.where(own_half, key_row[p : p + 1], value_row[p : p + 1])
        query = jnp.where(own_half, query_row[p : p + 1], 0.0)
        rows3[h] = jnp.where(at == 0, both, jnp.where(at == 1, query, 0.0))

    low8 = iota((8, LANES), 1) < HALF
    for p in range(PAIRS):
        row = iota((16, LANES), 0)
        offs = jnp.where(row < 8, off_ref[2 * p], off_ref[2 * p + 1])
        hot = onehot(iota((16, LANES), 1) == 16 * mod(row, 8) + offs)
        rows = []
        for ref in (k_few, v_few):
            got = nn(hot, ref[:, :, cols(p)].reshape(LANES, LANES))
            rows.append(jnp.where(low8, got[0:8], got[8:16]))
        pick2[p] = jnp.concatenate(rows, axis=0).astype(BF16)

    def select(p):
        row = iota((LANES, TOK), 0)
        low = iota((PICK, LANES), 1) < HALF
        offs = jnp.where(row < HALF, off_ref[2 * p], off_ref[2 * p + 1])
        hot = onehot(iota((LANES, TOK), 1) == 8 * mod(row, HALF) + offs)
        for n, ref in enumerate((k_ref, v_ref, q_ref)):
            got = nn(hot, all_of(ref, p))
            pick1[p, n * PICK : (n + 1) * PICK] = jnp.where(low, got[0:64], got[64:128]).astype(BF16)

    def own(p):
        v_up[p] = flipped(all_of(v_ref, p))
        for g in range(TOK // SPAN):
            rows = slice(g * SPAN, (g + 1) * SPAN)
            _, o = attend_t(rows_of(k_ref, g, p), stacked(rows_of(q_ref, g, p)), v_up[p, :, rows])
            a = o[0:64, 0:SPAN] / o[128:129, 0:SPAN]
            b = o[64:128, 0 + SPAN : 2 * SPAN] / o[128:129, SPAN : 2 * SPAN]
            up = jnp.concatenate([a, b], axis=0).astype(BF16)
            flat = nt(eye(SPAN), up)
            offs = jnp.where(iota((SPAN, LANES), 1) < HALF, off_ref[2 * p], off_ref[2 * p + 1])
            on = mod(iota((SPAN, LANES), 0), 8) == offs
            out_ref[rows, cols(p)] = jnp.where(on, 0.0, flat).astype(BF16)

    lane = iota((1, LANES), 1)

    def local_selected(p):
        qs = stacked(pick1[p, 2 * PICK : 3 * PICK])
        parts = []
        for g in range(TOK // SPAN):
            rows = slice(g * SPAN, (g + 1) * SPAN)
            parts.append(attend_t(rows_of(k_ref, g, p), qs, v_up[p, :, rows]))
        first = mod(lane, HALF) < PICK // 2
        top = jnp.where(first, parts[0][0], parts[1][0])
        o = jnp.where(first, parts[0][1], parts[1][1])
        sel_loc[p, 0:64] = jnp.where(lane < HALF, o[0:64], o[64:128])
        sel_loc[p, 64:72] = jnp.broadcast_to(top, (8, LANES))
        sel_loc[p, 72:80] = jnp.broadcast_to(o[128:129], (8, LANES))
        col = iota((TOK, LANES), 1)
        offs = jnp.where(col < HALF, off_ref[2 * p], off_ref[2 * p + 1])
        spread[p] = onehot(iota((TOK, LANES), 0) == 8 * mod(col, HALF) + offs)

    def local(p):
        own(p)
        local_selected(p)

    def loop(begin, end, body):
        lax.fori_loop(begin, end, lambda p, _: (body(p), 0)[1], 0)

    pl.semaphore_wait(barrier, 15 + 3 + 4 * z)

    def ring_at(g):
        return (div(g, 8) * 32 + mod(outer, 32), mod(g, 8))

    def ring_owner(h):
        return (h // PAIRS * 32 + mod(outer, 32), h % PAIRS + 1)

    def mine(h):
        return jnp.logical_and(owner, head == h)

    def ring_copy(h):
        return copy(rows3.at[h], ring3.at[ring], s_g.at[h], r_g.at[ring], ring_owner(h))

    def cell_copy(at):
        return copy(all3.at[cell], all3.at[cell], s_q.at[at], r_q.at[cell], at_cell(at))

    def back_copy(k):
        to = mod(ring + k, 16)
        return copy(ret3.at[to], got3.at[head], s_p.at[to], r_p.at[head], ring_at(to))

    for h in range(2 * PAIRS):
        pl.when(jnp.logical_not(mine(h)))(lambda: ring_copy(h).start())

        @pl.when(mine(h))
        def _(h=h):
            ring3[ring] = rows3[h]

    def send_a1(p):
        return copy(pick2.at[p], buf2.at[z, i], s_a1.at[p], r_a1.at[i], (outer, p + 1))

    def send_a2(p):
        return copy(pick1.at[p], buf1.at[i], s_a2.at[p], r_a2.at[i], (outer, p + 1))

    for p in range(PAIRS):
        @pl.when(i != p + 1)
        def _(p=p):
            send_a1(p).start()

        @pl.when(i == p + 1)
        def _(p=p):
            buf2[z, i] = pick2[p]

    cells(lambda at: pl.semaphore_signal(later, inc=1, device_id=at_cell(at), device_id_type=MESH), lambda w: w < z)

    for load in loads[3:]:
        load.wait()
    for p in range(PAIRS):
        select(p)

    for p in range(PAIRS):
        @pl.when(i != p + 1)
        def _(p=p):
            send_a2(p).start()

        @pl.when(i == p + 1)
        def _(p=p):
            buf1[i] = pick1[p]

    def z_send(buf, s, r, k):
        return copy(buf.at[z], buf.at[z], s.at[k], r.at[z], of_z(k))

    def z_recv(buf, s, r, k):
        other = mod(z + k, 8)
        return copy(buf.at[other], buf.at[other], s.at[k], r.at[other], of_z(k))

    loop(0, first_pairs, local)

    @pl.when(owner)
    def _():
        for k in range(1, 16):
            src = mod(ring + k, 16)
            copy(rows3.at[0], ring3.at[src], s_g.at[0], r_g.at[src], ring_at(src)).wait_recv()
        hot = onehot(iota((16, LANES), 1) == 8 * iota((16, LANES), 0))
        all3[cell] = nn(hot, ring3[...].reshape(LANES, LANES).astype(BF16)).astype(BF16)
        cells(lambda at: cell_copy(at).start(), lambda w: w <= z)
        for k in range(1, 8):
            src = mod(i + k, 8)
            copy(pick2.at[0], buf2.at[z, src], s_a1.at[0], r_a1.at[src], of_inner(k)).wait_recv()
        for k in (4, 3, 5, 2, 6, 1, 7):
            pl.when(mod(z + k, 8) < z)(lambda: z_send(buf2, s_b, r_b, k).start())

    pl.when(z < 7)(lambda: pl.semaphore_wait(later, 4 * (7 - z)))

    @pl.when(owner)
    def _():
        cells(lambda at: cell_copy(at).start(), lambda w: w > z)
        for k in (4, 3, 5, 2, 6, 1, 7):
            pl.when(mod(z + k, 8) > z)(lambda: z_send(buf2, s_b, r_b, k).start())

    loop(first_pairs, second_pairs, local)

    def level_one():
        keys = buf1[:, 0:PICK].reshape(8 * PICK, LANES)
        values = flipped(buf1[:, PICK : 2 * PICK].reshape(8 * PICK, LANES))
        for n in range(4):
            qs = jnp.concatenate([stacked(buf1[2 * n, 2 * PICK :]), stacked(buf1[2 * n + 1, 2 * PICK :])], axis=0)
            top, o = attend_t(keys, qs, values)
            total = o[128:129]
            parts = list(split3(top)) + list(split3(total)) + [jnp.zeros((10, 2 * LANES), F32)]
            both = mod(iota((1, 2 * LANES), 1), LANES) < HALF
            whole = jnp.concatenate([jnp.where(both, o[0:64], o[64:128])] + parts, axis=0).astype(BF16)
            ret1[2 * n] = whole[:, 0:LANES]
            ret1[2 * n + 1] = whole[:, LANES:]

    def ret_send(ret, got, s, r, k):
        dst = mod(i + k, 8)
        return copy(ret.at[dst], got.at[pair], s.at[k], r.at[pair], of_inner(k))

    @pl.when(owner)
    def _():
        for k in range(1, 8):
            src = mod(i + k, 8)
            copy(pick1.at[0], buf1.at[src], s_a2.at[0], r_a2.at[src], of_inner(k)).wait_recv()
        level_one()
        for k in range(1, 8):
            ret_send(ret1, got1, s_e, r_e, k).start()
        got1[pair] = ret1[i]

    @pl.when(owner)
    def _():
        for k in range(1, 32):
            at = mod(cell + k, 32)
            copy(all3.at[at], all3.at[at], s_q.at[at], r_q.at[at], at_cell(at)).wait_recv()
        hot = onehot(iota((16, LANES), 1) == 8 * iota((16, LANES), 0) + 1)
        queries = nn(hot, ring3[...].reshape(LANES, LANES).astype(BF16)).astype(BF16)
        rows = all3[...].reshape(TOK, LANES)
        s = nt(queries, rows)
        top = jnp.max(s, axis=1, keepdims=True)
        e = jnp.exp2((s - top) * COEF)
        total = jnp.sum(e, axis=1, keepdims=True)
        numer = nn(e.astype(BF16), rows)
        c = iota((16, LANES), 1)
        own_half = (c >= HALF) == odd
        spot = mod(c, HALF)
        stats = jnp.where(spot == 0, top, jnp.where(spot == 1, total, 0.0))
        whole = jnp.where(own_half, stats, numer)
        ret3[...] = jnp.broadcast_to(whole[:, None, :], (16, 8, LANES))
        for k in range(1, 16):
            back_copy(k).start()
        got3[head] = ret3[ring]

    def keys_values(buf):
        wide = buf[...].reshape(64, 16, LANES).astype(F32)
        return (wide[:, 0:8].reshape(512, LANES).astype(BF16), wide[:, 8:16].reshape(512, LANES).astype(BF16))

    def attend_rows(queries, buf):
        keys, values = keys_values(buf)
        s = nt(queries, keys)
        top = jnp.max(s, axis=1, keepdims=True)
        e = jnp.exp2((s - top) * COEF)
        return top, jnp.sum(e, axis=1, keepdims=True), nn(e.astype(BF16), values)

    @pl.when(owner)
    def _():
        r, c = iota((LANES, TOK), 0), iota((LANES, TOK), 1)
        hot = onehot(c == PICK * div(r, 16) + 8 * mod(r, 8))
        q2 = nn(hot, buf1[:, 2 * PICK :].reshape(TOK, LANES))
        r, c = iota((LANES, LANES), 0), iota((LANES, LANES), 1)
        mine = (mod(r, 16) < 8) == (c < HALF)
        q2 = jnp.where(mine, q2, 0.0).astype(BF16)
        for k in range(1, 8):
            z_recv(buf2, s_b, r_b, k).wait_recv()
        top2, total2, numer2 = attend_rows(q2, buf2)
        at = mod(c, HALF)
        whole = numer2
        for n, x in enumerate(split3(top2) + split3(total2)):
            whole = jnp.where(jnp.logical_and(jnp.logical_not(mine), at == n), x, whole)
        whole = jnp.where(jnp.logical_or(mine, at < 6), whole, 0.0)
        ret2[...] = whole.astype(BF16).reshape(8, 16, LANES)
        for k in range(1, 8):
            ret_send(ret2, got2, s_f, r_f, k).start()
        got2[pair] = ret2[i]

    loop(second_pairs, PAIRS, local)

    for p in range(PAIRS):
        @pl.when(i != p + 1)
        def _(p=p):
            copy(ret1.at[0], got1.at[p], s_e.at[1], r_e.at[p], (outer, p + 1)).wait_recv()

    for p in range(PAIRS):
        @pl.when(i != p + 1)
        def _(p=p):
            copy(ret2.at[0], got2.at[p], s_f.at[1], r_f.at[p], (outer, p + 1)).wait_recv()

    for h in range(2 * PAIRS):
        pl.when(jnp.logical_not(mine(h)))(
            lambda: copy(ret3.at[0], got3.at[h], s_p.at[0], r_p.at[h], ring_owner(h)).wait_recv()
        )
    at = iota((8, LANES), 0)
    halves = []
    for first_head in (0, 8):
        rows = jnp.zeros((8, LANES), F32)
        for h in range(first_head, min(first_head + 8, 2 * PAIRS)):
            rows = jnp.where(at == h - first_head, got3[h], rows)
        halves.append(rows)
    x = jnp.concatenate(halves, axis=0)
    r, c = iota((16, LANES), 0), iota((16, LANES), 1)
    own_half = mod(r, 2) == div(c, HALF)
    spot = mod(c, HALF)
    top = jnp.max(jnp.where(jnp.logical_and(own_half, spot == 0), x, NEG), axis=1, keepdims=True)
    total = jnp.sum(jnp.where(jnp.logical_and(own_half, spot == 1), x, 0.0), axis=1, keepdims=True)
    x = jnp.where(own_half, 0.0, x)
    for n, v in enumerate(split3(top) + split3(total)):
        x = jnp.where(jnp.logical_and(own_half, spot == n), v, x)
    rows4 = x.astype(BF16)
    r, c = iota((16, PAIRS * LANES), 0), iota((16, PAIRS * LANES), 1)
    all4 = tn(rows4, onehot(jnp.logical_and(r == div(c, HALF), mod(c, HALF) == 0)))

    r, c = iota((16, LANES), 0), iota((16, LANES), 1)
    hot = onehot(jnp.logical_and(div(r, 8) == div(c, HALF), mod(c, HALF) == 8 * mod(r, 8)))
    first = lane < HALF
    on = mod(lane, 8) == 0
    on4 = mod(lane, HALF) == 0

    def unpacked(x, first):
        st = jnp.where(first, x[64:72], x[0:8])
        return (st[0:1] + st[1:2]) + st[2:3], (st[3:4] + st[4:5]) + st[5:6], jnp.where(first, x[0:64], x[64:128])

    for p in range(PAIRS):
        top2, total2, numer2 = unpacked(tn(got2[p], hot), first)
        top3, total3, numer3 = unpacked(all4[:, cols(p)], jnp.logical_not(first))
        y = got1[p].astype(F32)
        numer1 = y[0:64]
        top1 = (y[64:65] + y[65:66]) + y[66:67]
        total1 = (y[67:68] + y[68:69]) + y[69:70]
        top0 = sel_loc[p, 64:65]
        total0 = sel_loc[p, 72:73]
        top2 = jnp.where(on, top2, top0)
        top3 = jnp.where(on4, top3, top0)
        peak = jnp.maximum(jnp.maximum(top0, top1), jnp.maximum(top2, top3))
        f0 = jnp.exp2((top0 - peak) * COEF)
        f1 = jnp.exp2((top1 - peak) * COEF)
        f2 = jnp.where(on, jnp.exp2((top2 - peak) * COEF), 0.0)
        f3 = jnp.where(on4, jnp.exp2((top3 - peak) * COEF), 0.0)
        total = f0 * total0 + f1 * total1 + f2 * total2 + f3 * total3
        done = (f0 * sel_loc[p, 0:64] + f1 * numer1 + f2 * numer2 + f3 * numer3) / total
        both = jnp.concatenate([jnp.where(first, done, 0.0), jnp.where(first, 0.0, done)], axis=0).astype(BF16)
        back = nt(spread[p], both)
        out_ref[:, cols(p)] = (out_ref[:, cols(p)].astype(F32) + back).astype(BF16)

    for h in range(2 * PAIRS):
        pl.when(jnp.logical_not(mine(h)))(lambda: ring_copy(h).wait_send())
    for p in range(PAIRS):
        @pl.when(i != p + 1)
        def _(p=p):
            send_a1(p).wait_send()
            send_a2(p).wait_send()

    @pl.when(owner)
    def _():
        for k in range(1, 8):
            z_send(buf2, s_b, r_b, k).wait_send()
            ret_send(ret1, got1, s_e, r_e, k).wait_send()
            ret_send(ret2, got2, s_f, r_f, k).wait_send()
        cells(lambda at: cell_copy(at).wait_send(), lambda w: w >= 0)
        for k in range(1, 16):
            back_copy(k).wait_send()


def shards(queries, keys, values, offsets, w_out):
    hbm = pl.BlockSpec(memory_space=pltpu.HBM)
    shape = (8, 64, queries.shape[1])
    dma = pltpu.SemaphoreType.DMA
    attended = pl.pallas_call(
        kernel,
        out_shape=jax.ShapeDtypeStruct(queries.shape, BF16),
        in_specs=[pl.BlockSpec(memory_space=pltpu.SMEM), hbm, hbm, hbm],
        out_specs=pl.BlockSpec(memory_space=pltpu.VMEM),
        scratch_shapes=[pltpu.VMEM(shape, BF16)] * 3 + [pltpu.VMEM((8, 16, shape[2]), BF16)] * 2 + [
            pltpu.VMEM((16, shape[2]), BF16),
            pltpu.VMEM((PAIRS, 16, LANES), BF16),
            pltpu.VMEM((PAIRS, 3 * PICK, LANES), BF16),
            pltpu.VMEM((8, 3 * PICK, LANES), BF16),
            pltpu.VMEM((8, 8, 16, LANES), BF16),
            pltpu.VMEM((8, 80, LANES), BF16),
            pltpu.VMEM((PAIRS, 80, LANES), BF16),
            pltpu.VMEM((8, 16, LANES), BF16),
            pltpu.VMEM((PAIRS, 16, LANES), BF16),
            pltpu.VMEM((2 * PAIRS, 8, LANES), F32),
            pltpu.VMEM((16, 8, LANES), F32),
            pltpu.VMEM((32, 16, LANES), BF16),
            pltpu.VMEM((16, 8, LANES), F32),
            pltpu.VMEM((2 * PAIRS, 8, LANES), F32),
            pltpu.VMEM((PAIRS, TOK, LANES), BF16),
            pltpu.VMEM((PAIRS, 144, TOK), BF16),
            pltpu.VMEM((PAIRS, 80, LANES), F32),
        ] + [dma((6,))] + [dma((8,))] * 10 + [dma((16,))] * 2 + [dma((32,))] * 4 + [pltpu.SemaphoreType.REGULAR],
        compiler_params=pltpu.CompilerParams(
            collective_id=0, has_side_effects=True, vmem_limit_bytes=53 * 1024 * 1024
        ),
    )(offsets, queries.reshape(shape), keys.reshape(shape), values.reshape(shape))
    return jnp.dot(attended, w_out, preferred_element_type=F32).astype(BF16)


def solution(mesh):
    rows = P(("outer", "inner"), None)
    return jax.shard_map(
        shards, mesh=mesh, in_specs=(rows, rows, rows, P(), P()), out_specs=rows, check_vma=False
    )
```

```python
import math

import jax
import jax.numpy as jnp
from jax import lax
from jax.experimental import pallas as pl
from jax.experimental.pallas import tpu as pltpu
from jax.sharding import PartitionSpec as P

MESH = pl.DeviceIdType.MESH
F32, BF16 = jnp.float32, jnp.bfloat16
LANES = 128
HALF = 64
SPAN = 256
TOK = 512
PICK = 64
PAIRS = 6
NEG = -1e30
COEF = 0.125 * math.log2(math.e)


def mod(x, n):
    return x & (n - 1)


def div(x, n):
    return x >> (n.bit_length() - 1)


def iota(shape, dim):
    return lax.broadcasted_iota(jnp.int32, shape, dim)


def nn(a, b):
    return lax.dot_general(a, b, (((1,), (0,)), ((), ())), preferred_element_type=F32)


def nt(a, b):
    return lax.dot_general(a, b, (((1,), (1,)), ((), ())), preferred_element_type=F32)


def tn(a, b):
    return lax.dot_general(a, b, (((0,), (0,)), ((), ())), preferred_element_type=F32)


def onehot(cond):
    return jnp.where(cond, jnp.float32(1), jnp.float32(0)).astype(BF16)


def eye(n):
    return onehot(iota((n, n), 0) == iota((n, n), 1))


def stacked(q):
    low = iota(q.shape, 1) < HALF
    wide = q.astype(F32)
    return jnp.concatenate([jnp.where(low, wide, 0.0), jnp.where(low, 0.0, wide)], axis=0).astype(BF16)


def split3(x):
    hi = x.astype(BF16).astype(F32)
    rest = x - hi
    mid = rest.astype(BF16).astype(F32)
    return hi, mid, rest - mid


def flipped(v):
    up = nt(eye(LANES), v)
    return jnp.concatenate([up, jnp.ones((16, v.shape[0]), F32)], axis=0).astype(BF16)


def attend_t(keys, queries, v_up):
    s = nt(keys, queries)
    top = jnp.max(s, axis=0, keepdims=True)
    w = jnp.exp2((s - top) * COEF).astype(BF16)
    return top, nn(v_up, w)


def kernel(off_hbm, q_hbm, k_hbm, v_hbm, out_ref, q_ref, k_ref, v_ref, k_few, v_few, q_few, pick2, pick1, buf1, buf2,
           ret1, got1, ret2, got2, rows3, ring3, all3, ret3, got3, spread, v_up, sel_loc, off_ref, s_in, s_a1, r_a1, s_a2, r_a2, s_b, r_b,
           s_e, r_e, s_f, r_f, s_g, r_g, s_q, r_q, s_p, r_p, later):
    outer = lax.axis_index("outer")
    i = lax.axis_index("inner")
    z = mod(outer, 8)
    xy = div(outer, 8)
    far = div(outer, 32)
    cell = z * 4 + mod(xy, 4)
    ring = far * 8 + i
    head = far * PAIRS + i - 1
    odd = mod(head, 2) == 1
    pair = i - 1
    owner = jnp.logical_and(i >= 1, i <= PAIRS)
    first_pairs = jnp.clip(7 - z, 1, PAIRS)
    second_pairs = jnp.maximum(first_pairs, 4)

    offsets = pltpu.make_async_copy(off_hbm, off_ref, s_in.at[6])
    offsets.start()
    loads = [pltpu.make_async_copy(hbm.at[:, pl.ds(0, 16)], few, s_in.at[n])
             for n, (hbm, few) in enumerate(((k_hbm, k_few), (v_hbm, v_few)))]
    loads += [pltpu.make_async_copy(q_hbm.at[0, pl.ds(0, 16)], q_few, s_in.at[2])]
    loads += [pltpu.make_async_copy(hbm, ref, s_in.at[3 + n])
              for n, (hbm, ref) in enumerate(((k_hbm, k_ref), (v_hbm, v_ref), (q_hbm, q_ref)))]
    for load in loads:
        load.start()

    def of_inner(k):
        return (outer, mod(i + k, 8))

    def of_z(k):
        return (xy * 8 + mod(z + k, 8), i)

    def at_cell(c):
        return (far * 32 + mod(c, 4) * 8 + div(c, 4), i)

    def of_cell(k):
        return at_cell(mod(cell + k, 32))

    def of_ring(k):
        at = mod(ring + k, 16)
        return (div(at, 8) * 32 + mod(outer, 32), mod(at, 8))

    barrier = pltpu.get_barrier_semaphore()
    for k in range(1, 16):
        pl.semaphore_signal(barrier, inc=1, device_id=of_ring(k), device_id_type=MESH)

    def cells(body, chosen):
        for k in range(1, 32):
            at = mod(cell + k, 32)
            pl.when(chosen(div(at, 4)))(lambda: body(at))

    cells(lambda at: pl.semaphore_signal(barrier, inc=1, device_id=at_cell(at), device_id_type=MESH), lambda w: w >= z)

    def cols(p):
        if isinstance(p, int):
            return slice(p * LANES, (p + 1) * LANES)
        return pl.ds(pl.multiple_of(p * LANES, LANES), LANES)

    def rows_of(ref, g, p):
        return ref[g * 4 : (g + 1) * 4, :, cols(p)].reshape(SPAN, LANES)

    def all_of(ref, p):
        return ref[:, :, cols(p)].reshape(TOK, LANES)

    def copy(src, dst, s, r, to):
        return pltpu.make_async_remote_copy(src_ref=src, dst_ref=dst, send_sem=s, recv_sem=r, device_id=to,
                                            device_id_type=MESH)

    offsets.wait()
    for load in loads[:3]:
        load.wait()

    def one_row(block):
        x = block.astype(F32)[0:8]
        at = iota((8, LANES), 0)
        rows = jnp.zeros((8, LANES), F32)
        for p in range(PAIRS):
            offs = jnp.where(iota((8, LANES), 1) < HALF, off_ref[2 * p], off_ref[2 * p + 1])
            row = jnp.sum(jnp.where(at == offs, x[:, cols(p)], 0.0), axis=0, keepdims=True)
            rows = jnp.where(at == p, row, rows)
        return rows

    key_row, value_row, query_row = one_row(k_few[0]), pltpu.roll(one_row(v_few[0]), HALF, 1), one_row(q_few[...])
    at, low = iota((8, LANES), 0), iota((8, LANES), 1) < HALF
    for h in range(2 * PAIRS):
        p = div(h, 2)
        own_half = low if h % 2 == 0 else jnp.logical_not(low)
        both = jnp.where(own_half, key_row[p : p + 1], value_row[p : p + 1])
        query = jnp.where(own_half, query_row[p : p + 1], 0.0)
        rows3[h] = jnp.where(at == 0, both, jnp.where(at == 1, query, 0.0))

    low8 = iota((8, LANES), 1) < HALF
    for p in range(PAIRS):
        row = iota((16, LANES), 0)
        offs = jnp.where(row < 8, off_ref[2 * p], off_ref[2 * p + 1])
        hot = onehot(iota((16, LANES), 1) == 16 * mod(row, 8) + offs)
        rows = []
        for ref in (k_few, v_few):
            got = nn(hot, ref[:, :, cols(p)].reshape(LANES, LANES))
            rows.append(jnp.where(low8, got[0:8], got[8:16]))
        pick2[p] = jnp.concatenate(rows, axis=0).astype(BF16)

    def select(p):
        row = iota((LANES, TOK), 0)
        low = iota((PICK, LANES), 1) < HALF
        offs = jnp.where(row < HALF, off_ref[2 * p], off_ref[2 * p + 1])
        hot = onehot(iota((LANES, TOK), 1) == 8 * mod(row, HALF) + offs)
        for n, ref in enumerate((k_ref, v_ref, q_ref)):
            got = nn(hot, all_of(ref, p))
            pick1[p, n * PICK : (n + 1) * PICK] = jnp.where(low, got[0:64], got[64:128]).astype(BF16)

    def own(p):
        v_up[p] = flipped(all_of(v_ref, p))
        for g in range(TOK // SPAN):
            rows = slice(g * SPAN, (g + 1) * SPAN)
            _, o = attend_t(rows_of(k_ref, g, p), stacked(rows_of(q_ref, g, p)), v_up[p, :, rows])
            a = o[0:64, 0:SPAN] / o[128:129, 0:SPAN]
            b = o[64:128, 0 + SPAN : 2 * SPAN] / o[128:129, SPAN : 2 * SPAN]
            up = jnp.concatenate([a, b], axis=0).astype(BF16)
            flat = nt(eye(SPAN), up)
            offs = jnp.where(iota((SPAN, LANES), 1) < HALF, off_ref[2 * p], off_ref[2 * p + 1])
            on = mod(iota((SPAN, LANES), 0), 8) == offs
            out_ref[rows, cols(p)] = jnp.where(on, 0.0, flat).astype(BF16)

    lane = iota((1, LANES), 1)

    def local_selected(p):
        qs = stacked(pick1[p, 2 * PICK : 3 * PICK])
        parts = []
        for g in range(TOK // SPAN):
            rows = slice(g * SPAN, (g + 1) * SPAN)
            parts.append(attend_t(rows_of(k_ref, g, p), qs, v_up[p, :, rows]))
        first = mod(lane, HALF) < PICK // 2
        top = jnp.where(first, parts[0][0], parts[1][0])
        o = jnp.where(first, parts[0][1], parts[1][1])
        sel_loc[p, 0:64] = jnp.where(lane < HALF, o[0:64], o[64:128])
        sel_loc[p, 64:72] = jnp.broadcast_to(top, (8, LANES))
        sel_loc[p, 72:80] = jnp.broadcast_to(o[128:129], (8, LANES))
        col = iota((TOK, LANES), 1)
        offs = jnp.where(col < HALF, off_ref[2 * p], off_ref[2 * p + 1])
        spread[p] = onehot(iota((TOK, LANES), 0) == 8 * mod(col, HALF) + offs)

    def local(p):
        own(p)
        local_selected(p)

    def loop(begin, end, body):
        lax.fori_loop(begin, end, lambda p, _: (body(p), 0)[1], 0)

    pl.semaphore_wait(barrier, 15 + 3 + 4 * z)

    def ring_at(g):
        return (div(g, 8) * 32 + mod(outer, 32), mod(g, 8))

    def ring_owner(h):
        return (h // PAIRS * 32 + mod(outer, 32), h % PAIRS + 1)

    def mine(h):
        return jnp.logical_and(owner, head == h)

    def ring_copy(h):
        return copy(rows3.at[h], ring3.at[ring], s_g.at[h], r_g.at[ring], ring_owner(h))

    def cell_copy(at):
        return copy(all3.at[cell], all3.at[cell], s_q.at[at], r_q.at[cell], at_cell(at))

    def back_copy(k):
        to = mod(ring + k, 16)
        return copy(ret3.at[to], got3.at[head], s_p.at[to], r_p.at[head], ring_at(to))

    for h in range(2 * PAIRS):
        pl.when(jnp.logical_not(mine(h)))(lambda: ring_copy(h).start())

        @pl.when(mine(h))
        def _(h=h):
            ring3[ring] = rows3[h]

    def send_a1(p):
        return copy(pick2.at[p], buf2.at[z, i], s_a1.at[p], r_a1.at[i], (outer, p + 1))

    def send_a2(p):
        return copy(pick1.at[p], buf1.at[i], s_a2.at[p], r_a2.at[i], (outer, p + 1))

    for p in range(PAIRS):
        @pl.when(i != p + 1)
        def _(p=p):
            send_a1(p).start()

        @pl.when(i == p + 1)
        def _(p=p):
            buf2[z, i] = pick2[p]

    cells(lambda at: pl.semaphore_signal(later, inc=1, device_id=at_cell(at), device_id_type=MESH), lambda w: w < z)

    for load in loads[3:]:
        load.wait()
    for p in range(PAIRS):
        select(p)

    for p in range(PAIRS):
        @pl.when(i != p + 1)
        def _(p=p):
            send_a2(p).start()

        @pl.when(i == p + 1)
        def _(p=p):
            buf1[i] = pick1[p]

    def z_send(buf, s, r, k):
        return copy(buf.at[z], buf.at[z], s.at[k], r.at[z], of_z(k))

    def z_recv(buf, s, r, k):
        other = mod(z + k, 8)
        return copy(buf.at[other], buf.at[other], s.at[k], r.at[other], of_z(k))

    loop(0, first_pairs, local)

    @pl.when(owner)
    def _():
        for k in range(1, 16):
            src = mod(ring + k, 16)
            copy(rows3.at[0], ring3.at[src], s_g.at[0], r_g.at[src], ring_at(src)).wait_recv()
        hot = onehot(iota((16, LANES), 1) == 8 * iota((16, LANES), 0))
        all3[cell] = nn(hot, ring3[...].reshape(LANES, LANES).astype(BF16)).astype(BF16)
        cells(lambda at: cell_copy(at).start(), lambda w: w <= z)
        for k in range(1, 8):
            src = mod(i + k, 8)
            copy(pick2.at[0], buf2.at[z, src], s_a1.at[0], r_a1.at[src], of_inner(k)).wait_recv()
        for to in range(7):
            pl.when(to < z)(lambda: z_send(buf2, s_b, r_b, mod(to - z + 8, 8)).start())

    pl.when(z < 7)(lambda: pl.semaphore_wait(later, 4 * (7 - z)))

    @pl.when(owner)
    def _():
        cells(lambda at: cell_copy(at).start(), lambda w: w > z)
        for to in range(1, 8):
            pl.when(to > z)(lambda: z_send(buf2, s_b, r_b, mod(to - z + 8, 8)).start())

    loop(first_pairs, second_pairs, local)

    def level_one():
        keys = buf1[:, 0:PICK].reshape(8 * PICK, LANES)
        values = flipped(buf1[:, PICK : 2 * PICK].reshape(8 * PICK, LANES))
        for n in range(4):
            qs = jnp.concatenate([stacked(buf1[2 * n, 2 * PICK :]), stacked(buf1[2 * n + 1, 2 * PICK :])], axis=0)
            top, o = attend_t(keys, qs, values)
            total = o[128:129]
            parts = list(split3(top)) + list(split3(total)) + [jnp.zeros((10, 2 * LANES), F32)]
            both = mod(iota((1, 2 * LANES), 1), LANES) < HALF
            whole = jnp.concatenate([jnp.where(both, o[0:64], o[64:128])] + parts, axis=0).astype(BF16)
            ret1[2 * n] = whole[:, 0:LANES]
            ret1[2 * n + 1] = whole[:, LANES:]

    def ret_send(ret, got, s, r, k):
        dst = mod(i + k, 8)
        return copy(ret.at[dst], got.at[pair], s.at[k], r.at[pair], of_inner(k))

    @pl.when(owner)
    def _():
        for k in range(1, 8):
            src = mod(i + k, 8)
            copy(pick1.at[0], buf1.at[src], s_a2.at[0], r_a2.at[src], of_inner(k)).wait_recv()
        level_one()
        for k in range(1, 8):
            ret_send(ret1, got1, s_e, r_e, k).start()
        got1[pair] = ret1[i]

    @pl.when(owner)
    def _():
        for k in range(1, 32):
            at = mod(cell + k, 32)
            copy(all3.at[at], all3.at[at], s_q.at[at], r_q.at[at], at_cell(at)).wait_recv()
        hot = onehot(iota((16, LANES), 1) == 8 * iota((16, LANES), 0) + 1)
        queries = nn(hot, ring3[...].reshape(LANES, LANES).astype(BF16)).astype(BF16)
        rows = all3[...].reshape(TOK, LANES)
        s = nt(queries, rows)
        top = jnp.max(s, axis=1, keepdims=True)
        e = jnp.exp2((s - top) * COEF)
        total = jnp.sum(e, axis=1, keepdims=True)
        numer = nn(e.astype(BF16), rows)
        c = iota((16, LANES), 1)
        own_half = (c >= HALF) == odd
        spot = mod(c, HALF)
        stats = jnp.where(spot == 0, top, jnp.where(spot == 1, total, 0.0))
        whole = jnp.where(own_half, stats, numer)
        ret3[...] = jnp.broadcast_to(whole[:, None, :], (16, 8, LANES))
        for k in range(1, 16):
            back_copy(k).start()
        got3[head] = ret3[ring]

    def keys_values(buf):
        wide = buf[...].reshape(64, 16, LANES).astype(F32)
        return (wide[:, 0:8].reshape(512, LANES).astype(BF16), wide[:, 8:16].reshape(512, LANES).astype(BF16))

    def attend_rows(queries, buf):
        keys, values = keys_values(buf)
        s = nt(queries, keys)
        top = jnp.max(s, axis=1, keepdims=True)
        e = jnp.exp2((s - top) * COEF)
        return top, jnp.sum(e, axis=1, keepdims=True), nn(e.astype(BF16), values)

    @pl.when(owner)
    def _():
        r, c = iota((LANES, TOK), 0), iota((LANES, TOK), 1)
        hot = onehot(c == PICK * div(r, 16) + 8 * mod(r, 8))
        q2 = nn(hot, buf1[:, 2 * PICK :].reshape(TOK, LANES))
        r, c = iota((LANES, LANES), 0), iota((LANES, LANES), 1)
        mine = (mod(r, 16) < 8) == (c < HALF)
        q2 = jnp.where(mine, q2, 0.0).astype(BF16)
        for k in range(1, 8):
            z_recv(buf2, s_b, r_b, k).wait_recv()
        top2, total2, numer2 = attend_rows(q2, buf2)
        at = mod(c, HALF)
        whole = numer2
        for n, x in enumerate(split3(top2) + split3(total2)):
            whole = jnp.where(jnp.logical_and(jnp.logical_not(mine), at == n), x, whole)
        whole = jnp.where(jnp.logical_or(mine, at < 6), whole, 0.0)
        ret2[...] = whole.astype(BF16).reshape(8, 16, LANES)
        for k in range(1, 8):
            ret_send(ret2, got2, s_f, r_f, k).start()
        got2[pair] = ret2[i]

    loop(second_pairs, PAIRS, local)

    for p in range(PAIRS):
        @pl.when(i != p + 1)
        def _(p=p):
            copy(ret1.at[0], got1.at[p], s_e.at[1], r_e.at[p], (outer, p + 1)).wait_recv()

    for h in range(2 * PAIRS):
        pl.when(jnp.logical_not(mine(h)))(lambda: ring_copy(h).wait_send())
    for p in range(PAIRS):
        @pl.when(i != p + 1)
        def _(p=p):
            send_a1(p).wait_send()
            send_a2(p).wait_send()

    @pl.when(owner)
    def _():
        for k in range(1, 8):
            z_send(buf2, s_b, r_b, k).wait_send()
            ret_send(ret1, got1, s_e, r_e, k).wait_send()
            ret_send(ret2, got2, s_f, r_f, k).wait_send()
        cells(lambda at: cell_copy(at).wait_send(), lambda w: w >= 0)
        for k in range(1, 16):
            back_copy(k).wait_send()

    first = lane < HALF
    for p in range(PAIRS):
        y = got1[p].astype(F32)
        top1 = (y[64:65] + y[65:66]) + y[66:67]
        total1 = (y[67:68] + y[68:69]) + y[69:70]
        top0 = sel_loc[p, 64:65]
        peak = jnp.maximum(top0, top1)
        f0 = jnp.exp2((top0 - peak) * COEF)
        f1 = jnp.exp2((top1 - peak) * COEF)
        total = f0 * sel_loc[p, 72:73] + f1 * total1
        sel_loc[p, 0:64] = f0 * sel_loc[p, 0:64] + f1 * y[0:64]
        sel_loc[p, 64:72] = jnp.broadcast_to(peak, (8, LANES))
        sel_loc[p, 72:80] = jnp.broadcast_to(total, (8, LANES))

    for p in range(PAIRS):
        @pl.when(i != p + 1)
        def _(p=p):
            copy(ret2.at[0], got2.at[p], s_f.at[1], r_f.at[p], (outer, p + 1)).wait_recv()

    for h in range(2 * PAIRS):
        pl.when(jnp.logical_not(mine(h)))(
            lambda: copy(ret3.at[0], got3.at[h], s_p.at[0], r_p.at[h], ring_owner(h)).wait_recv()
        )
    at = iota((8, LANES), 0)
    halves = []
    for first_head in (0, 8):
        rows = jnp.zeros((8, LANES), F32)
        for h in range(first_head, min(first_head + 8, 2 * PAIRS)):
            rows = jnp.where(at == h - first_head, got3[h], rows)
        halves.append(rows)
    x = jnp.concatenate(halves, axis=0)
    r, c = iota((16, LANES), 0), iota((16, LANES), 1)
    own_half = mod(r, 2) == div(c, HALF)
    spot = mod(c, HALF)
    top = jnp.max(jnp.where(jnp.logical_and(own_half, spot == 0), x, NEG), axis=1, keepdims=True)
    total = jnp.sum(jnp.where(jnp.logical_and(own_half, spot == 1), x, 0.0), axis=1, keepdims=True)
    x = jnp.where(own_half, 0.0, x)
    for n, v in enumerate(split3(top) + split3(total)):
        x = jnp.where(jnp.logical_and(own_half, spot == n), v, x)
    rows4 = x.astype(BF16)
    r, c = iota((16, PAIRS * LANES), 0), iota((16, PAIRS * LANES), 1)
    all4 = tn(rows4, onehot(jnp.logical_and(r == div(c, HALF), mod(c, HALF) == 0)))

    r, c = iota((16, LANES), 0), iota((16, LANES), 1)
    hot = onehot(jnp.logical_and(div(r, 8) == div(c, HALF), mod(c, HALF) == 8 * mod(r, 8)))
    on = mod(lane, 8) == 0
    on4 = mod(lane, HALF) == 0

    def unpacked(x, first):
        st = jnp.where(first, x[64:72], x[0:8])
        return (st[0:1] + st[1:2]) + st[2:3], (st[3:4] + st[4:5]) + st[5:6], jnp.where(first, x[0:64], x[64:128])

    for p in range(PAIRS):
        top2, total2, numer2 = unpacked(tn(got2[p], hot), first)
        top3, total3, numer3 = unpacked(all4[:, cols(p)], jnp.logical_not(first))
        top0 = sel_loc[p, 64:65]
        top2 = jnp.where(on, top2, top0)
        top3 = jnp.where(on4, top3, top0)
        peak = jnp.maximum(top0, jnp.maximum(top2, top3))
        f0 = jnp.exp2((top0 - peak) * COEF)
        f2 = jnp.where(on, jnp.exp2((top2 - peak) * COEF), 0.0)
        f3 = jnp.where(on4, jnp.exp2((top3 - peak) * COEF), 0.0)
        total = f0 * sel_loc[p, 72:73] + f2 * total2 + f3 * total3
        done = (f0 * sel_loc[p, 0:64] + f2 * numer2 + f3 * numer3) / total
        both = jnp.concatenate([jnp.where(first, done, 0.0), jnp.where(first, 0.0, done)], axis=0).astype(BF16)
        back = nt(spread[p], both)
        out_ref[:, cols(p)] = (out_ref[:, cols(p)].astype(F32) + back).astype(BF16)


def shards(queries, keys, values, offsets, w_out):
    hbm = pl.BlockSpec(memory_space=pltpu.HBM)
    shape = (8, 64, queries.shape[1])
    dma = pltpu.SemaphoreType.DMA
    attended = pl.pallas_call(
        kernel,
        out_shape=jax.ShapeDtypeStruct(queries.shape, BF16),
        in_specs=[hbm] * 4,
        out_specs=pl.BlockSpec(memory_space=pltpu.VMEM),
        scratch_shapes=[pltpu.VMEM(shape, BF16)] * 3 + [pltpu.VMEM((8, 16, shape[2]), BF16)] * 2 + [
            pltpu.VMEM((16, shape[2]), BF16),
            pltpu.VMEM((PAIRS, 16, LANES), BF16),
            pltpu.VMEM((PAIRS, 3 * PICK, LANES), BF16),
            pltpu.VMEM((8, 3 * PICK, LANES), BF16),
            pltpu.VMEM((8, 8, 16, LANES), BF16),
            pltpu.VMEM((8, 80, LANES), BF16),
            pltpu.VMEM((PAIRS, 80, LANES), BF16),
            pltpu.VMEM((8, 16, LANES), BF16),
            pltpu.VMEM((PAIRS, 16, LANES), BF16),
            pltpu.VMEM((2 * PAIRS, 8, LANES), F32),
            pltpu.VMEM((16, 8, LANES), F32),
            pltpu.VMEM((32, 16, LANES), BF16),
            pltpu.VMEM((16, 8, LANES), F32),
            pltpu.VMEM((2 * PAIRS, 8, LANES), F32),
            pltpu.VMEM((PAIRS, TOK, LANES), BF16),
            pltpu.VMEM((PAIRS, 144, TOK), BF16),
            pltpu.VMEM((PAIRS, 80, LANES), F32),
            pltpu.SMEM(offsets.shape, jnp.int32),
        ] + [dma((7,))] + [dma((8,))] * 10 + [dma((16,))] * 2 + [dma((32,))] * 4 + [pltpu.SemaphoreType.REGULAR],
        compiler_params=pltpu.CompilerParams(
            collective_id=0, has_side_effects=True, vmem_limit_bytes=53 * 1024 * 1024
        ),
    )(offsets, queries.reshape(shape), keys.reshape(shape), values.reshape(shape))
    return jnp.dot(attended, w_out, preferred_element_type=F32).astype(BF16)


def solution(mesh):
    rows = P(("outer", "inner"), None)
    return jax.shard_map(
        shards, mesh=mesh, in_specs=(rows, rows, rows, P(), P()), out_specs=rows, check_vma=False
    )
```

```python
import math

import jax
import jax.numpy as jnp
from jax import lax
from jax.experimental import pallas as pl
from jax.experimental.pallas import tpu as pltpu
from jax.sharding import PartitionSpec as P

MESH = pl.DeviceIdType.MESH
F32, BF16 = jnp.float32, jnp.bfloat16
LANES = 128
HALF = 64
SPAN = 256
TOK = 512
PICK = 64
PAIRS = 6
NEG = -1e30
COEF = 0.125 * math.log2(math.e)


def mod(x, n):
    return x & (n - 1)


def div(x, n):
    return x >> (n.bit_length() - 1)


def iota(shape, dim):
    return lax.broadcasted_iota(jnp.int32, shape, dim)


def nn(a, b):
    return lax.dot_general(a, b, (((1,), (0,)), ((), ())), preferred_element_type=F32)


def nt(a, b):
    return lax.dot_general(a, b, (((1,), (1,)), ((), ())), preferred_element_type=F32)


def tn(a, b):
    return lax.dot_general(a, b, (((0,), (0,)), ((), ())), preferred_element_type=F32)


def onehot(cond):
    return jnp.where(cond, jnp.float32(1), jnp.float32(0)).astype(BF16)


def eye(n):
    return onehot(iota((n, n), 0) == iota((n, n), 1))


def stacked(q):
    low = iota(q.shape, 1) < HALF
    wide = q.astype(F32)
    return jnp.concatenate([jnp.where(low, wide, 0.0), jnp.where(low, 0.0, wide)], axis=0).astype(BF16)


def split3(x):
    hi = x.astype(BF16).astype(F32)
    rest = x - hi
    mid = rest.astype(BF16).astype(F32)
    return hi, mid, rest - mid


def flipped(v):
    up = nt(eye(LANES), v)
    return jnp.concatenate([up, jnp.ones((16, v.shape[0]), F32)], axis=0).astype(BF16)


def attend_t(keys, queries, v_up):
    s = nt(keys, queries)
    top = jnp.max(s, axis=0, keepdims=True)
    w = jnp.exp2((s - top) * COEF).astype(BF16)
    return top, nn(v_up, w)


def kernel(off_hbm, q_hbm, k_hbm, v_hbm, out_ref, q_ref, k_ref, v_ref, k_few, v_few, q_few, pick2, pick1, buf1, buf2,
           ret1, got1, ret2, got2, rows3, ring3, all3, ret3, got3, spread, v_up, sel_loc, off_ref, s_in, s_a1, r_a1, s_a2, r_a2, s_b, r_b,
           s_e, r_e, s_f, r_f, s_g, r_g, s_q, r_q, s_p, r_p, later):
    outer = lax.axis_index("outer")
    i = lax.axis_index("inner")
    z = mod(outer, 8)
    xy = div(outer, 8)
    far = div(outer, 32)
    cell = z * 4 + mod(xy, 4)
    ring = far * 8 + i
    head = far * PAIRS + i - 1
    odd = mod(head, 2) == 1
    pair = i - 1
    owner = jnp.logical_and(i >= 1, i <= PAIRS)
    first_pairs = jnp.clip(6 - z, 0, PAIRS)
    second_pairs = jnp.maximum(first_pairs, 4)

    offsets = pltpu.make_async_copy(off_hbm, off_ref, s_in.at[6])
    offsets.start()
    loads = [pltpu.make_async_copy(hbm.at[:, pl.ds(0, 16)], few, s_in.at[n])
             for n, (hbm, few) in enumerate(((k_hbm, k_few), (v_hbm, v_few)))]
    loads += [pltpu.make_async_copy(q_hbm.at[0, pl.ds(0, 16)], q_few, s_in.at[2])]
    loads += [pltpu.make_async_copy(hbm, ref, s_in.at[3 + n])
              for n, (hbm, ref) in enumerate(((k_hbm, k_ref), (v_hbm, v_ref), (q_hbm, q_ref)))]
    for load in loads:
        load.start()

    def of_inner(k):
        return (outer, mod(i + k, 8))

    def of_z(k):
        return (xy * 8 + mod(z + k, 8), i)

    def at_cell(c):
        return (far * 32 + mod(c, 4) * 8 + div(c, 4), i)

    def of_cell(k):
        return at_cell(mod(cell + k, 32))

    def of_ring(k):
        at = mod(ring + k, 16)
        return (div(at, 8) * 32 + mod(outer, 32), mod(at, 8))

    barrier = pltpu.get_barrier_semaphore()
    for k in range(1, 16):
        pl.semaphore_signal(barrier, inc=1, device_id=of_ring(k), device_id_type=MESH)

    def cells(body, chosen):
        for k in range(1, 32):
            at = mod(cell + k, 32)
            pl.when(chosen(div(at, 4)))(lambda: body(at))

    cells(lambda at: pl.semaphore_signal(barrier, inc=1, device_id=at_cell(at), device_id_type=MESH), lambda w: w >= z)

    def cols(p):
        if isinstance(p, int):
            return slice(p * LANES, (p + 1) * LANES)
        return pl.ds(pl.multiple_of(p * LANES, LANES), LANES)

    def rows_of(ref, g, p):
        return ref[g * 4 : (g + 1) * 4, :, cols(p)].reshape(SPAN, LANES)

    def all_of(ref, p):
        return ref[:, :, cols(p)].reshape(TOK, LANES)

    def copy(src, dst, s, r, to):
        return pltpu.make_async_remote_copy(src_ref=src, dst_ref=dst, send_sem=s, recv_sem=r, device_id=to,
                                            device_id_type=MESH)

    offsets.wait()
    for load in loads[:3]:
        load.wait()

    def one_row(block):
        x = block.astype(F32)[0:8]
        at = iota((8, LANES), 0)
        rows = jnp.zeros((8, LANES), F32)
        for p in range(PAIRS):
            offs = jnp.where(iota((8, LANES), 1) < HALF, off_ref[2 * p], off_ref[2 * p + 1])
            row = jnp.sum(jnp.where(at == offs, x[:, cols(p)], 0.0), axis=0, keepdims=True)
            rows = jnp.where(at == p, row, rows)
        return rows

    key_row, value_row, query_row = one_row(k_few[0]), pltpu.roll(one_row(v_few[0]), HALF, 1), one_row(q_few[...])
    at, low = iota((8, LANES), 0), iota((8, LANES), 1) < HALF
    for h in range(2 * PAIRS):
        p = div(h, 2)
        own_half = low if h % 2 == 0 else jnp.logical_not(low)
        both = jnp.where(own_half, key_row[p : p + 1], value_row[p : p + 1])
        query = jnp.where(own_half, query_row[p : p + 1], 0.0)
        rows3[h] = jnp.where(at == 0, both, jnp.where(at == 1, query, 0.0))

    low8 = iota((8, LANES), 1) < HALF
    for p in range(PAIRS):
        row = iota((16, LANES), 0)
        offs = jnp.where(row < 8, off_ref[2 * p], off_ref[2 * p + 1])
        hot = onehot(iota((16, LANES), 1) == 16 * mod(row, 8) + offs)
        rows = []
        for ref in (k_few, v_few):
            got = nn(hot, ref[:, :, cols(p)].reshape(LANES, LANES))
            rows.append(jnp.where(low8, got[0:8], got[8:16]))
        pick2[p] = jnp.concatenate(rows, axis=0).astype(BF16)

    def select(p):
        row = iota((LANES, TOK), 0)
        low = iota((PICK, LANES), 1) < HALF
        offs = jnp.where(row < HALF, off_ref[2 * p], off_ref[2 * p + 1])
        hot = onehot(iota((LANES, TOK), 1) == 8 * mod(row, HALF) + offs)
        for n, ref in enumerate((k_ref, v_ref, q_ref)):
            got = nn(hot, all_of(ref, p))
            pick1[p, n * PICK : (n + 1) * PICK] = jnp.where(low, got[0:64], got[64:128]).astype(BF16)

    def own(p):
        v_up[p] = flipped(all_of(v_ref, p))
        for g in range(TOK // SPAN):
            rows = slice(g * SPAN, (g + 1) * SPAN)
            _, o = attend_t(rows_of(k_ref, g, p), stacked(rows_of(q_ref, g, p)), v_up[p, :, rows])
            a = o[0:64, 0:SPAN] / o[128:129, 0:SPAN]
            b = o[64:128, 0 + SPAN : 2 * SPAN] / o[128:129, SPAN : 2 * SPAN]
            up = jnp.concatenate([a, b], axis=0).astype(BF16)
            flat = nt(eye(SPAN), up)
            offs = jnp.where(iota((SPAN, LANES), 1) < HALF, off_ref[2 * p], off_ref[2 * p + 1])
            on = mod(iota((SPAN, LANES), 0), 8) == offs
            out_ref[rows, cols(p)] = jnp.where(on, 0.0, flat).astype(BF16)

    lane = iota((1, LANES), 1)

    def local_selected(p):
        qs = stacked(pick1[p, 2 * PICK : 3 * PICK])
        parts = []
        for g in range(TOK // SPAN):
            rows = slice(g * SPAN, (g + 1) * SPAN)
            parts.append(attend_t(rows_of(k_ref, g, p), qs, v_up[p, :, rows]))
        first = mod(lane, HALF) < PICK // 2
        top = jnp.where(first, parts[0][0], parts[1][0])
        o = jnp.where(first, parts[0][1], parts[1][1])
        sel_loc[p, 0:64] = jnp.where(lane < HALF, o[0:64], o[64:128])
        sel_loc[p, 64:72] = jnp.broadcast_to(top, (8, LANES))
        sel_loc[p, 72:80] = jnp.broadcast_to(o[128:129], (8, LANES))
        col = iota((TOK, LANES), 1)
        offs = jnp.where(col < HALF, off_ref[2 * p], off_ref[2 * p + 1])
        spread[p] = onehot(iota((TOK, LANES), 0) == 8 * mod(col, HALF) + offs)

    def local(p):
        own(p)
        local_selected(p)

    def loop(begin, end, body):
        lax.fori_loop(begin, end, lambda p, _: (body(p), 0)[1], 0)

    pl.semaphore_wait(barrier, 15 + 3 + 4 * z)

    def ring_at(g):
        return (div(g, 8) * 32 + mod(outer, 32), mod(g, 8))

    def ring_owner(h):
        return (h // PAIRS * 32 + mod(outer, 32), h % PAIRS + 1)

    def mine(h):
        return jnp.logical_and(owner, head == h)

    def ring_copy(h):
        return copy(rows3.at[h], ring3.at[ring], s_g.at[h], r_g.at[ring], ring_owner(h))

    def cell_copy(at):
        return copy(all3.at[cell], all3.at[cell], s_q.at[at], r_q.at[cell], at_cell(at))

    def back_copy(k):
        to = mod(ring + k, 16)
        return copy(ret3.at[to], got3.at[head], s_p.at[to], r_p.at[head], ring_at(to))

    for h in range(2 * PAIRS):
        pl.when(jnp.logical_not(mine(h)))(lambda: ring_copy(h).start())

        @pl.when(mine(h))
        def _(h=h):
            ring3[ring] = rows3[h]

    def send_a1(p):
        return copy(pick2.at[p], buf2.at[z, i], s_a1.at[p], r_a1.at[i], (outer, p + 1))

    def send_a2(p):
        return copy(pick1.at[p], buf1.at[i], s_a2.at[p], r_a2.at[i], (outer, p + 1))

    for p in range(PAIRS):
        @pl.when(i != p + 1)
        def _(p=p):
            send_a1(p).start()

        @pl.when(i == p + 1)
        def _(p=p):
            buf2[z, i] = pick2[p]

    cells(lambda at: pl.semaphore_signal(later, inc=1, device_id=at_cell(at), device_id_type=MESH), lambda w: w < z)

    for load in loads[3:]:
        load.wait()
    for p in range(PAIRS):
        select(p)

    def deal():
        for p in range(PAIRS):
            pl.when(i != p + 1)(lambda: send_a2(p).start())

            @pl.when(i == p + 1)
            def _(p=p):
                buf1[i] = pick1[p]

    pl.when(z < 4)(deal)

    def z_send(buf, s, r, k):
        return copy(buf.at[z], buf.at[z], s.at[k], r.at[z], of_z(k))

    def z_recv(buf, s, r, k):
        other = mod(z + k, 8)
        return copy(buf.at[other], buf.at[other], s.at[k], r.at[other], of_z(k))

    loop(0, first_pairs, local)

    @pl.when(owner)
    def _():
        for k in range(1, 16):
            src = mod(ring + k, 16)
            copy(rows3.at[0], ring3.at[src], s_g.at[0], r_g.at[src], ring_at(src)).wait_recv()
        hot = onehot(iota((16, LANES), 1) == 8 * iota((16, LANES), 0))
        all3[cell] = nn(hot, ring3[...].reshape(LANES, LANES).astype(BF16)).astype(BF16)
        cells(lambda at: cell_copy(at).start(), lambda w: w <= z)
        for k in range(1, 8):
            src = mod(i + k, 8)
            copy(pick2.at[0], buf2.at[z, src], s_a1.at[0], r_a1.at[src], of_inner(k)).wait_recv()
        for to in range(7):
            pl.when(to < z)(lambda: z_send(buf2, s_b, r_b, mod(to - z + 8, 8)).start())

    pl.when(z >= 4)(deal)

    pl.when(z < 7)(lambda: pl.semaphore_wait(later, 4 * (7 - z)))

    @pl.when(owner)
    def _():
        cells(lambda at: cell_copy(at).start(), lambda w: w > z)
        for to in range(1, 8):
            pl.when(to > z)(lambda: z_send(buf2, s_b, r_b, mod(to - z + 8, 8)).start())

    loop(first_pairs, second_pairs, local)

    def level_one():
        keys = buf1[:, 0:PICK].reshape(8 * PICK, LANES)
        values = flipped(buf1[:, PICK : 2 * PICK].reshape(8 * PICK, LANES))
        for n in range(4):
            qs = jnp.concatenate([stacked(buf1[2 * n, 2 * PICK :]), stacked(buf1[2 * n + 1, 2 * PICK :])], axis=0)
            top, o = attend_t(keys, qs, values)
            total = o[128:129]
            parts = list(split3(top)) + list(split3(total)) + [jnp.zeros((10, 2 * LANES), F32)]
            both = mod(iota((1, 2 * LANES), 1), LANES) < HALF
            whole = jnp.concatenate([jnp.where(both, o[0:64], o[64:128])] + parts, axis=0).astype(BF16)
            ret1[2 * n] = whole[:, 0:LANES]
            ret1[2 * n + 1] = whole[:, LANES:]

    def ret_send(ret, got, s, r, k):
        dst = mod(i + k, 8)
        return copy(ret.at[dst], got.at[pair], s.at[k], r.at[pair], of_inner(k))

    @pl.when(owner)
    def _():
        for k in range(1, 8):
            src = mod(i + k, 8)
            copy(pick1.at[0], buf1.at[src], s_a2.at[0], r_a2.at[src], of_inner(k)).wait_recv()
        level_one()
        for k in range(1, 8):
            ret_send(ret1, got1, s_e, r_e, k).start()
        got1[pair] = ret1[i]

    @pl.when(owner)
    def _():
        hot = onehot(iota((16, LANES), 1) == 8 * iota((16, LANES), 0) + 1)
        queries = nn(hot, ring3[...].reshape(LANES, LANES).astype(BF16)).astype(BF16)
        for k in range(1, 32):
            at = mod(cell + k, 32)
            copy(all3.at[at], all3.at[at], s_q.at[at], r_q.at[at], at_cell(at)).wait_recv()
        rows = all3[...].reshape(TOK, LANES)
        s = nt(queries, rows)
        top = jnp.max(s, axis=1, keepdims=True)
        e = jnp.exp2((s - top) * COEF)
        total = jnp.sum(e, axis=1, keepdims=True)
        numer = nn(e.astype(BF16), rows)
        c = iota((16, LANES), 1)
        own_half = (c >= HALF) == odd
        spot = mod(c, HALF)
        stats = jnp.where(spot == 0, top, jnp.where(spot == 1, total, 0.0))
        whole = jnp.where(own_half, stats, numer)
        ret3[...] = jnp.broadcast_to(whole[:, None, :], (16, 8, LANES))
        for k in range(1, 16):
            back_copy(k).start()
        got3[head] = ret3[ring]

    def keys_values(buf):
        wide = buf[...].reshape(64, 16, LANES).astype(F32)
        return (wide[:, 0:8].reshape(512, LANES).astype(BF16), wide[:, 8:16].reshape(512, LANES).astype(BF16))

    def attend_rows(queries, buf):
        keys, values = keys_values(buf)
        s = nt(queries, keys)
        top = jnp.max(s, axis=1, keepdims=True)
        e = jnp.exp2((s - top) * COEF)
        return top, jnp.sum(e, axis=1, keepdims=True), nn(e.astype(BF16), values)

    @pl.when(owner)
    def _():
        r, c = iota((LANES, TOK), 0), iota((LANES, TOK), 1)
        hot = onehot(c == PICK * div(r, 16) + 8 * mod(r, 8))
        q2 = nn(hot, buf1[:, 2 * PICK :].reshape(TOK, LANES))
        r, c = iota((LANES, LANES), 0), iota((LANES, LANES), 1)
        mine = (mod(r, 16) < 8) == (c < HALF)
        q2 = jnp.where(mine, q2, 0.0).astype(BF16)
        for k in range(1, 8):
            z_recv(buf2, s_b, r_b, k).wait_recv()
        top2, total2, numer2 = attend_rows(q2, buf2)
        at = mod(c, HALF)
        whole = numer2
        for n, x in enumerate(split3(top2) + split3(total2)):
            whole = jnp.where(jnp.logical_and(jnp.logical_not(mine), at == n), x, whole)
        whole = jnp.where(jnp.logical_or(mine, at < 6), whole, 0.0)
        ret2[...] = whole.astype(BF16).reshape(8, 16, LANES)
        for k in range(1, 8):
            ret_send(ret2, got2, s_f, r_f, k).start()
        got2[pair] = ret2[i]

    loop(second_pairs, PAIRS, local)

    for p in range(PAIRS):
        @pl.when(i != p + 1)
        def _(p=p):
            copy(ret1.at[0], got1.at[p], s_e.at[1], r_e.at[p], (outer, p + 1)).wait_recv()

    for h in range(2 * PAIRS):
        pl.when(jnp.logical_not(mine(h)))(lambda: ring_copy(h).wait_send())
    for p in range(PAIRS):
        @pl.when(i != p + 1)
        def _(p=p):
            send_a1(p).wait_send()
            send_a2(p).wait_send()

    @pl.when(owner)
    def _():
        for k in range(1, 8):
            z_send(buf2, s_b, r_b, k).wait_send()
            ret_send(ret1, got1, s_e, r_e, k).wait_send()
            ret_send(ret2, got2, s_f, r_f, k).wait_send()
        cells(lambda at: cell_copy(at).wait_send(), lambda w: w >= 0)
        for k in range(1, 16):
            back_copy(k).wait_send()

    first = lane < HALF
    for p in range(PAIRS):
        y = got1[p].astype(F32)
        top1 = (y[64:65] + y[65:66]) + y[66:67]
        total1 = (y[67:68] + y[68:69]) + y[69:70]
        top0 = sel_loc[p, 64:65]
        peak = jnp.maximum(top0, top1)
        f0 = jnp.exp2((top0 - peak) * COEF)
        f1 = jnp.exp2((top1 - peak) * COEF)
        total = f0 * sel_loc[p, 72:73] + f1 * total1
        sel_loc[p, 0:64] = f0 * sel_loc[p, 0:64] + f1 * y[0:64]
        sel_loc[p, 64:72] = jnp.broadcast_to(peak, (8, LANES))
        sel_loc[p, 72:80] = jnp.broadcast_to(total, (8, LANES))

    for p in range(PAIRS):
        @pl.when(i != p + 1)
        def _(p=p):
            copy(ret2.at[0], got2.at[p], s_f.at[1], r_f.at[p], (outer, p + 1)).wait_recv()

    def unpacked(x, first):
        st = jnp.where(first, x[64:72], x[0:8])
        return (st[0:1] + st[1:2]) + st[2:3], (st[3:4] + st[4:5]) + st[5:6], jnp.where(first, x[0:64], x[64:128])

    r, c = iota((16, LANES), 0), iota((16, LANES), 1)
    hot = onehot(jnp.logical_and(div(r, 8) == div(c, HALF), mod(c, HALF) == 8 * mod(r, 8)))
    on = mod(lane, 8) == 0
    for p in range(PAIRS):
        top2, total2, numer2 = unpacked(tn(got2[p], hot), first)
        top0 = sel_loc[p, 64:65]
        top2 = jnp.where(on, top2, top0)
        peak = jnp.maximum(top0, top2)
        f0 = jnp.exp2((top0 - peak) * COEF)
        f2 = jnp.where(on, jnp.exp2((top2 - peak) * COEF), 0.0)
        total = f0 * sel_loc[p, 72:73] + f2 * total2
        sel_loc[p, 0:64] = f0 * sel_loc[p, 0:64] + f2 * numer2
        sel_loc[p, 64:72] = jnp.broadcast_to(peak, (8, LANES))
        sel_loc[p, 72:80] = jnp.broadcast_to(total, (8, LANES))

    for h in range(2 * PAIRS):
        pl.when(jnp.logical_not(mine(h)))(
            lambda: copy(ret3.at[0], got3.at[h], s_p.at[0], r_p.at[h], ring_owner(h)).wait_recv()
        )
    at = iota((8, LANES), 0)
    halves = []
    for first_head in (0, 8):
        rows = jnp.zeros((8, LANES), F32)
        for h in range(first_head, min(first_head + 8, 2 * PAIRS)):
            rows = jnp.where(at == h - first_head, got3[h], rows)
        halves.append(rows)
    x = jnp.concatenate(halves, axis=0)
    r, c = iota((16, LANES), 0), iota((16, LANES), 1)
    own_half = mod(r, 2) == div(c, HALF)
    spot = mod(c, HALF)
    top = jnp.max(jnp.where(jnp.logical_and(own_half, spot == 0), x, NEG), axis=1, keepdims=True)
    total = jnp.sum(jnp.where(jnp.logical_and(own_half, spot == 1), x, 0.0), axis=1, keepdims=True)
    x = jnp.where(own_half, 0.0, x)
    for n, v in enumerate(split3(top) + split3(total)):
        x = jnp.where(jnp.logical_and(own_half, spot == n), v, x)
    rows4 = x.astype(BF16)
    r, c = iota((16, PAIRS * LANES), 0), iota((16, PAIRS * LANES), 1)
    all4 = tn(rows4, onehot(jnp.logical_and(r == div(c, HALF), mod(c, HALF) == 0)))

    on4 = mod(lane, HALF) == 0

    for p in range(PAIRS):
        top3, total3, numer3 = unpacked(all4[:, cols(p)], jnp.logical_not(first))
        top0 = sel_loc[p, 64:65]
        top3 = jnp.where(on4, top3, top0)
        peak = jnp.maximum(top0, top3)
        f0 = jnp.exp2((top0 - peak) * COEF)
        f3 = jnp.where(on4, jnp.exp2((top3 - peak) * COEF), 0.0)
        total = f0 * sel_loc[p, 72:73] + f3 * total3
        done = (f0 * sel_loc[p, 0:64] + f3 * numer3) / total
        both = jnp.concatenate([jnp.where(first, done, 0.0), jnp.where(first, 0.0, done)], axis=0).astype(BF16)
        back = nt(spread[p], both)
        out_ref[:, cols(p)] = (out_ref[:, cols(p)].astype(F32) + back).astype(BF16)


def shards(queries, keys, values, offsets, w_out):
    hbm = pl.BlockSpec(memory_space=pltpu.HBM)
    shape = (8, 64, queries.shape[1])
    dma = pltpu.SemaphoreType.DMA
    attended = pl.pallas_call(
        kernel,
        out_shape=jax.ShapeDtypeStruct(queries.shape, BF16),
        in_specs=[hbm] * 4,
        out_specs=pl.BlockSpec(memory_space=pltpu.VMEM),
        scratch_shapes=[pltpu.VMEM(shape, BF16)] * 3 + [pltpu.VMEM((8, 16, shape[2]), BF16)] * 2 + [
            pltpu.VMEM((16, shape[2]), BF16),
            pltpu.VMEM((PAIRS, 16, LANES), BF16),
            pltpu.VMEM((PAIRS, 3 * PICK, LANES), BF16),
            pltpu.VMEM((8, 3 * PICK, LANES), BF16),
            pltpu.VMEM((8, 8, 16, LANES), BF16),
            pltpu.VMEM((8, 80, LANES), BF16),
            pltpu.VMEM((PAIRS, 80, LANES), BF16),
            pltpu.VMEM((8, 16, LANES), BF16),
            pltpu.VMEM((PAIRS, 16, LANES), BF16),
            pltpu.VMEM((2 * PAIRS, 8, LANES), F32),
            pltpu.VMEM((16, 8, LANES), F32),
            pltpu.VMEM((32, 16, LANES), BF16),
            pltpu.VMEM((16, 8, LANES), F32),
            pltpu.VMEM((2 * PAIRS, 8, LANES), F32),
            pltpu.VMEM((PAIRS, TOK, LANES), BF16),
            pltpu.VMEM((PAIRS, 144, TOK), BF16),
            pltpu.VMEM((PAIRS, 80, LANES), F32),
            pltpu.SMEM(offsets.shape, jnp.int32),
        ] + [dma((7,))] + [dma((8,))] * 10 + [dma((16,))] * 2 + [dma((32,))] * 4 + [pltpu.SemaphoreType.REGULAR],
        compiler_params=pltpu.CompilerParams(
            collective_id=0, has_side_effects=True, vmem_limit_bytes=53 * 1024 * 1024
        ),
    )(offsets, queries.reshape(shape), keys.reshape(shape), values.reshape(shape))
    return jnp.dot(attended, w_out, preferred_element_type=F32).astype(BF16)


def solution(mesh):
    rows = P(("outer", "inner"), None)
    return jax.shard_map(
        shards, mesh=mesh, in_specs=(rows, rows, rows, P(), P()), out_specs=rows, check_vma=False
    )
```
